768 devices in a mesh: row: 96 (over z, x, y_hi), col: 8 (over y_lo, core).
Axes of the slice: x: 4, y: 8 (y_hi: 2, y_lo: 4; y = y_hi * 4 + y_lo), z: 12, core: 2. Of those that a mesh axis runs over, the one named last changes fastest.
Arguments:
- x_band: float32 [288, 13, 128, 128], P('row', None, 'col'), may hold values from -0.48 to 0.48
- x_mask: int32 [288, 13], P('row'), may hold values 0 or 1
- sq_mask: int32 [288, 19], P('row'), may hold values 0 or 1
- cube_mask: int32 [288, 25], P('row'), may hold values 0 or 1
Outputs:
- purified: float32 [288, 25, 128, 128], P('row', None, 'col')
The draws below stay inside these ranges and needn't reach their ends.
All inputs are finite; a program needn't handle non-finite values. No bound on the sum of `x_mask` or of `sq_mask` or of `cube_mask` on one device may be relied on, other than what follows from the above.
Results may differ from the reference program's by a relative error of at most 0.0001.
Values sent between devices are 32-bit elements; how exact they have to be, the bound alone decides.
No kernel may reach another device: no remote copies, remote signals or barrier semaphores. Data moves between devices by JAX's collectives and lax.ppermute only.
A program may use at most 32 MiB of HBM per device.

```python
import jax
import jax.numpy as jnp
from jax import lax

B = 128
HALF_X = 6
HALF_SQ = 9
HALF_CUBE = 12
NB = 288


def set_ends(array, key, low, top_value):
    shape = array.shape
    index_at = [jax.random.randint(jax.random.fold_in(key, axis), (), 0, shape[axis]) for axis in range(len(shape))]
    array = array.at[tuple(index_at)].set(low)
    longest = shape.index(max(shape))
    index_at[longest] = (index_at[longest] + 1) % shape[longest]
    return array.at[tuple(index_at)].set(top_value)


def block_levels(own_key, shape, cuts, least, largest):
    loudness = 1.0
    for position, parts in cuts:
        heights = jax.random.uniform(jax.random.fold_in(jax.random.fold_in(own_key, 6), position), (parts,), jnp.float32, least / len(cuts), largest / len(cuts))
        loudness = loudness * jnp.repeat(jnp.exp(heights), shape[position] // parts).reshape((-1,) + (1,) * (len(shape) - 1 - position))
    return loudness


def centred(rng, shape, scale, most, pieces=(), held_as=jnp.bfloat16):
    entries = scale * jax.random.normal(rng, shape, jnp.float32)
    if pieces:
        entries = entries * block_levels(rng, shape, pieces, -0.22, 0.18)
    return jnp.clip(entries, -most, most).astype(held_as)


def setup_inputs(seed: int = 0) -> dict:
    seeds = jax.random.split(jax.random.key(seed), 5)
    return {
        "x_band": centred(seeds[0], (NB, 2 * HALF_X + 1, B, B), 0.08, 0.48, ((0, 96), (2, 8)), jnp.float32),
        "x_mask": set_ends((jax.random.randint(seeds[1], (NB, 2 * HALF_X + 1), 0, 8) < 7).astype(jnp.int32), jax.random.fold_in(seeds[1], 1), 0, 1),
        "sq_mask": set_ends((jax.random.randint(seeds[2], (NB, 2 * HALF_SQ + 1), 0, 4) < 3).astype(jnp.int32), jax.random.fold_in(seeds[2], 1), 0, 1),
        "cube_mask": set_ends((jax.random.randint(seeds[3], (NB, 2 * HALF_CUBE + 1), 0, 4) < 3).astype(jnp.int32), jax.random.fold_in(seeds[3], 1), 0, 1),
    }


def band_apply(whole, left_band, half_right, half_left, half_out):
    summed = None
    for offset_left in range(-half_left, half_left + 1):
        lowest = max(-half_out, offset_left - half_right)
        highest = min(half_out, offset_left + half_right)
        first_slot = lowest - offset_left + half_right
        right_slab = jnp.roll(whole[:, first_slot:first_slot + highest - lowest + 1], -offset_left, axis=0)
        product = jnp.einsum("gojk,gki->goji", right_slab, left_band[:, offset_left + half_left], precision=lax.Precision.HIGHEST)
        placed = jnp.pad(product, ((0, 0), (lowest + half_out, half_out - highest), (0, 0), (0, 0)))
        summed = placed if summed is None else summed + placed
    return summed


def reference(x_band, x_mask, sq_mask, cube_mask):
    masked = x_band * x_mask[:, :, None, None].astype(jnp.float32)
    square = band_apply(masked, masked, HALF_X, HALF_X, HALF_SQ)
    square = square * sq_mask[:, :, None, None].astype(jnp.float32)
    cube = band_apply(masked, square, HALF_X, HALF_SQ, HALF_CUBE)
    widened = jnp.pad(square, ((0, 0), (HALF_CUBE - HALF_SQ, HALF_CUBE - HALF_SQ), (0, 0), (0, 0)))
    return (3.0 * widened - 2.0 * cube) * cube_mask[:, :, None, None].astype(jnp.float32)
```

```python
import jax
import jax.numpy as jnp
from jax import lax
from jax.experimental import pallas as pl
from jax.experimental.pallas import tpu as pltpu
from jax.sharding import PartitionSpec as P

Z, X, YH, YL, CORES = 12, 4, 2, 4, 2
CHAIN = Z * X
AXES = ("row", "col")
F32, BF16 = jnp.float32, jnp.bfloat16
VMEM_LIMIT = 48 * 1024 * 1024


def pairs(target):
    listed = []
    for c in range(CHAIN):
        for yh in range(YH):
            for yl in range(YL):
                for core in range(CORES):
                    to = target(c, yh, yl, core)
                    if to is not None:
                        tc, th, tl, tk = to
                        source = ((c * YH + yh) * YL + yl) * CORES + core
                        listed.append((source, (((tc % CHAIN) * YH + th) * YL + tl) * CORES + tk))
    return listed


UP = pairs(lambda c, h, l, k: (c + 1, h, l, k))
DOWN = pairs(lambda c, h, l, k: (c - 1, h, l, k))
ACROSS = pairs(lambda c, h, l, k: (c + 1 if h == 0 else c - 1, h, l, k))
AGAINST = pairs(lambda c, h, l, k: (c - 1 if h == 0 else c + 1, h, l, k))
FLIP = pairs(lambda c, h, l, k: (c, 1 - h, 3 - l, k))
MIRROR = pairs(lambda c, h, l, k: (c, h, 3 - l, k))
NEXT = pairs(lambda c, h, l, k: (c, h, l ^ 1, k))
SIBLING = pairs(lambda c, h, l, k: (c, h, l, 1 - k))


def send(array, which):
    return lax.ppermute(array, AXES, which)


def split(values):
    high = values.astype(BF16)
    return high, (values - high.astype(F32)).astype(BF16)


def mask_kernel(mask_ref, x_ref, out_ref):
    for g in range(x_ref.shape[0]):
        for d in range(x_ref.shape[1]):
            out_ref[g, d] = x_ref[g, d] * mask_ref[g, d].astype(F32)


def fill_window(place_ref, rows, first_place, high_ref, low_ref):
    for n, ref in enumerate(rows):
        base = place_ref[first_place + n] * 3
        for j in range(3):
            high, low = split(ref[j].reshape(high_ref.shape[1:]))
            high_ref[base + j] = high
            low_ref[base + j] = low


def fill_right(place_ref, slabs, first_place, pad, high_ref, low_ref):
    count = slabs[0].shape[1]
    blank = jnp.zeros((pad, 128, 128), BF16)
    for g in range(3):
        for ref in (high_ref, low_ref):
            ref[g, 0:pad] = blank
            ref[g, pad + count : 2 * pad + count] = blank
    for n, slab in enumerate(slabs):
        at = pl.ds(pl.multiple_of(place_ref[first_place + n] * 16, 16), 16)
        for g in range(3):
            high, low = split(slab[g])
            high_ref[g, pad : pad + count, at, :] = high
            low_ref[g, pad : pad + count, at, :] = low


def accumulate(window_rows, window_high, window_low, right_high, right_low, total_ref):
    total_ref[...] = jnp.zeros_like(total_ref)

    @pl.loop(0, window_rows)
    def _(r):
        left_high, left_low = window_high[r], window_low[r]
        highs = [right_high[g, r + 2 - g] for g in range(3)]
        lows = [right_low[g, r + 2 - g] for g in range(3)]
        wide_high = jnp.concatenate(highs, axis=1)
        wide_low = jnp.concatenate(lows, axis=1)
        product = jnp.dot(
            jnp.concatenate([left_high, left_low], axis=1),
            jnp.concatenate([wide_high, wide_high], axis=0),
            preferred_element_type=F32,
        ) + jnp.dot(left_high, wide_low, preferred_element_type=F32)
        product = product.reshape(13, 16, 384)
        for g in range(3):
            total_ref[g, pl.ds(r + 2 - g, 13)] += product[:, :, 128 * g : 128 * (g + 1)]


def square_kernel(place_ref, mask_ref, *refs):
    rows, slabs = refs[0:5], refs[5:13]
    out_ref, window_high, window_low, right_high, right_low, total_ref = refs[13:]
    fill_window(place_ref, rows, 0, window_high, window_low)
    fill_right(place_ref, slabs, 5, 2, right_high, right_low)
    accumulate(15, window_high, window_low, right_high, right_low, total_ref)
    for g in range(3):
        for e in range(19):
            out_ref[g, e] = total_ref[g, e + 5] * mask_ref[g, e].astype(F32)


def cube_kernel(place_ref, mask_ref, *refs):
    rows, slabs = refs[0:7], refs[7:15]
    out_ref, window_high, window_low, right_high, right_low, total_ref = refs[15:]
    own = slabs[0]
    fill_window(place_ref, rows, 0, window_high, window_low)
    fill_right(place_ref, slabs, 7, 2, right_high, right_low)
    accumulate(21, window_high, window_low, right_high, right_low, total_ref)
    for g in range(3):
        for f in range(25):
            value = -2.0 * total_ref[g, f + 5]
            if 3 <= f < 22:
                value = 3.0 * own[g, f - 3] + value
            out_ref[g, f] = value * mask_ref[g, f].astype(F32)


SMEM = pl.BlockSpec(memory_space=pltpu.SMEM)
VMEM = pl.BlockSpec(memory_space=pltpu.VMEM)


def banded(kernel, places, mask, arrays, window_rows, blocks_right, blocks_out, flops):
    return pl.pallas_call(
        kernel,
        out_shape=jax.ShapeDtypeStruct((3, mask.shape[1], 16, 128), F32),
        in_specs=[SMEM, SMEM] + [VMEM] * len(arrays),
        out_specs=VMEM,
        scratch_shapes=[
            pltpu.VMEM((window_rows, 13 * 16, 128), BF16),
            pltpu.VMEM((window_rows, 13 * 16, 128), BF16),
            pltpu.VMEM((3, blocks_right + 4, 128, 128), BF16),
            pltpu.VMEM((3, blocks_right + 4, 128, 128), BF16),
            pltpu.VMEM((3, blocks_out, 16, 128), F32),
        ],
        compiler_params=pltpu.CompilerParams(vmem_limit_bytes=VMEM_LIMIT),
        cost_estimate=pl.CostEstimate(
            flops=flops, bytes_accessed=4 * sum(a.size for a in arrays), transcendentals=0
        ),
    )(places, mask, *arrays)


def body(x_band, x_mask, sq_mask, cube_mask):
    high_y = lax.axis_index("row") % 2
    low_y, core = lax.axis_index("col") // 2, lax.axis_index("col") % 2

    own = pl.pallas_call(
        mask_kernel,
        out_shape=jax.ShapeDtypeStruct(x_band.shape, F32),
        in_specs=[SMEM, VMEM],
        out_specs=VMEM,
    )(x_mask, x_band)

    pair_m = send(own, FLIP)
    own_m = send(own, MIRROR)
    below_o, above_o = send(own, UP), send(own, DOWN)
    pair_o = send(pair_m, MIRROR)
    next_o, next_m = send(own, NEXT), send(own_m, NEXT)
    below_m, above_m = send(own_m, UP), send(own_m, DOWN)
    beside_m = send(pair_m, ACROSS)
    beside_o = send(pair_o, ACROSS)
    far_a = send(pair_o, AGAINST)
    far_b = send(beside_o, ACROSS)

    chips = jnp.stack([low_y, 3 - low_y, low_y ^ 1, (3 - low_y) ^ 1])
    orbitals = jnp.concatenate([2 * chips + core, 2 * chips + 1 - core])
    pair_at, beside_at = 3 - 2 * high_y, 1 + 2 * high_y
    square_rows = jnp.stack([jnp.int32(0), jnp.int32(4), jnp.int32(2), pair_at, beside_at])
    square_places = jnp.concatenate([square_rows, orbitals]).astype(jnp.int32)

    left = [own, own_m, next_o, next_m]
    left += [send(a, SIBLING) for a in left]
    square_flops = 2 * 3 * 45 * 208 * 128 * 128

    def square_of(rows):
        return banded(square_kernel, square_places, sq_mask, rows + left, 15, 13, 29, square_flops)

    square_m = square_of([below_m, above_m, own_m, pair_m, beside_m])
    square_o = square_of([below_o, above_o, own, pair_o, beside_o])

    right = [square_o, square_m, send(square_o, NEXT), send(square_m, NEXT)]
    right += [send(a, SIBLING) for a in right]
    cube_rows = [1, 5, 3, pair_at + 1, beside_at + 1, 6 - 6 * high_y, 6 * high_y]
    cube_places = jnp.concatenate([jnp.stack([jnp.int32(v) for v in cube_rows]), orbitals])
    cube_places = cube_places.astype(jnp.int32)
    rows = [below_o, above_o, own, pair_o, beside_o, far_a, far_b]
    return banded(
        cube_kernel, cube_places, cube_mask, rows + right, 21, 19, 35, 2 * 3 * 63 * 208 * 128 * 128
    )


def solution(mesh):
    return jax.shard_map(
        body,
        mesh=mesh,
        in_specs=(P("row", None, "col", None), P("row", None), P("row", None), P("row", None)),
        out_specs=P("row", None, "col", None),
        check_vma=False,
    )
```

```python
import functools

import jax
import jax.numpy as jnp
from jax import lax
from jax.experimental import pallas as pl
from jax.experimental.pallas import tpu as pltpu
from jax.sharding import PartitionSpec as P

Z, X, YH, YL, CORES = 12, 4, 2, 4, 2
CHAIN = Z * X
AXES = ("row", "col")
F32, BF16 = jnp.float32, jnp.bfloat16


def pairs(target):
    listed = []
    for c in range(CHAIN):
        for yh in range(YH):
            for yl in range(YL):
                for core in range(CORES):
                    to = target(c, yh, yl, core)
                    if to is not None:
                        tc, th, tl, tk = to
                        source = ((c * YH + yh) * YL + yl) * CORES + core
                        listed.append((source, (((tc % CHAIN) * YH + th) * YL + tl) * CORES + tk))
    return listed


UP = pairs(lambda c, h, l, k: (c + 1, h, l, k))
DOWN = pairs(lambda c, h, l, k: (c - 1, h, l, k))
ACROSS = pairs(lambda c, h, l, k: (c + 1 if h == 0 else c - 1, h, l, k))
AGAINST = pairs(lambda c, h, l, k: (c - 1 if h == 0 else c + 1, h, l, k))
FLIP = pairs(lambda c, h, l, k: (c, 1 - h, 3 - l, k))
MIRROR = pairs(lambda c, h, l, k: (c, h, 3 - l, k))
NEXT = pairs(lambda c, h, l, k: (c, h, l ^ 1, k))
SIBLING = pairs(lambda c, h, l, k: (c, h, l, 1 - k))


def send(array, which):
    return lax.ppermute(array, AXES, which)


def together(*arrays):
    return lax.optimization_barrier(arrays)


def split(values):
    high = values.astype(BF16)
    return high, (values - high.astype(F32)).astype(BF16)


def mask_kernel(mask_ref, x_ref, out_ref):
    for g in range(x_ref.shape[0]):
        for d in range(x_ref.shape[1]):
            out_ref[g, d] = x_ref[g, d] * mask_ref[g, d].astype(F32)


def lanes(g):
    return slice(128 * g, 128 * (g + 1))


def blank_corners(right_ref, blocks):
    for g in range(3):
        for r in range(blocks + 2):
            if not 0 <= r - g < blocks:
                right_ref[r, :, lanes(g)] = jnp.zeros((right_ref.shape[1], 128), BF16)


def put_right(right_ref, at, slab):
    blocks = slab.shape[1]
    for g in range(3):
        high, low = split(slab[g])
        for first, is_high in at:
            spot = pl.ds(pl.multiple_of(first, 16), 16)
            right_ref[g : g + blocks, spot, lanes(g)] = high if is_high else low


def accumulate(window_ref, right_ref, total_ref):
    for r in range(window_ref.shape[0]):
        product = jnp.dot(window_ref[r], right_ref[r], preferred_element_type=F32)
        product = product.reshape(13, 16, 384)
        for g in range(3):
            total_ref[g, r + 2 - g : r + 15 - g] += product[:, :, lanes(g)]


def viewed(refs, views):
    return [refs[n] if part is None else refs[n].at[part] for n, part in views]


def square_kernel(views, arrays, place_ref, mask_ref, *refs):
    given = viewed(refs, views)
    rows, slabs = given[:5], given[5:]
    out_ref, window_ref, right_ref, total_ref = refs[arrays:]
    for n, ref in enumerate(rows):
        base = place_ref[n] * 3
        for j in range(3):
            high, low = split(ref[j].reshape(208, 128))
            for part, value in enumerate((high, low, high)):
                window_ref[base + j, :, lanes(part)] = value
    blank_corners(right_ref, 13)
    for n, slab in enumerate(slabs):
        at = place_ref[5 + n] * 16
        put_right(right_ref, ((at, True), (128 + at, True), (256 + at, False)), slab)
    total_ref[...] = jnp.zeros_like(total_ref)
    accumulate(window_ref, right_ref, total_ref)
    for g in range(3):
        for e in range(19):
            out_ref[g, e] = total_ref[g, e + 5] * mask_ref[g, e].astype(F32)


def fill_half(right_ref, chips, slabs, core):
    blank_corners(right_ref, 19)
    zero = jnp.zeros((21, 16, 384), BF16)
    for n, chip in enumerate(chips):
        other = lax.rem(chip + 2, 4)
        for k in range(2):
            right_ref[:, pl.ds(pl.multiple_of(128 + 32 * other + 16 * k, 16), 16), :] = zero
        for k, slab in ((core, slabs[n]), (1 - core, slabs[2 + n])):
            place = 32 * chip + 16 * k
            again = 32 * other + 16 * k
            put_right(right_ref, ((place, True), (again, True), (128 + place, False)), slab)


def cube_first_kernel(views, arrays, place_ref, *refs):
    given = viewed(refs, views)
    rows, slabs = given[:7], given[7:]
    total_ref, next_ref, window_ref, right_ref = refs[arrays:]
    low_y, core = place_ref[7], place_ref[8]
    chip = lax.broadcasted_iota(jnp.int32, (208, 128), 1) // 32
    mine = (chip == low_y) | (chip == 3 - low_y)
    for n, ref in enumerate(rows):
        base = place_ref[n] * 3
        for j in range(3):
            values = ref[j].reshape(208, 128)
            rounded = values.astype(BF16)
            high = rounded.astype(F32)
            low = pltpu.roll(values - high, 64, 1)
            window_ref[base + j, :, lanes(0)] = jnp.where(mine, high, low).astype(BF16)
            window_ref[base + j, :, lanes(1)] = rounded
            next_ref[base + j, :, lanes(0)] = jnp.where(mine, low, high).astype(BF16)
            next_ref[base + j, :, lanes(1)] = rounded
    fill_half(right_ref, (low_y, 3 - low_y), slabs, core)
    total_ref[...] = jnp.zeros_like(total_ref)
    accumulate(window_ref, right_ref, total_ref)


def cube_second_kernel(views, arrays, place_ref, mask_ref, *refs):
    given = viewed(refs, views)
    before_ref, window_ref, own_ref, slabs = given[0], given[1], given[2], given[3:]
    out_ref, right_ref, total_ref = refs[arrays:]
    low_y, core = place_ref[7], place_ref[8]
    fill_half(right_ref, (low_y ^ 1, (3 - low_y) ^ 1), slabs, core)
    total_ref[...] = before_ref[...]
    accumulate(window_ref, right_ref, total_ref)
    for g in range(3):
        for f in range(25):
            value = -2.0 * total_ref[g, f + 5]
            if 3 <= f < 22:
                value = 3.0 * own_ref[g, f - 3] + value
            out_ref[g, f] = value * mask_ref[g, f].astype(F32)


SMEM = pl.BlockSpec(memory_space=pltpu.SMEM)
VMEM = pl.BlockSpec(memory_space=pltpu.VMEM)
ANYWHERE = pl.BlockSpec(memory_space=pl.ANY)
MIB = 1024 * 1024


def call(kernel, scalars, given, out_shape, scratch, limit, micros, after=()):
    arrays, views = [], []
    for item in given:
        array, part = item if isinstance(item, tuple) else (item, None)
        held = [n for n, known in enumerate(arrays) if known is array]
        if not held:
            arrays.append(array)
        views.append((held[0] if held else len(arrays) - 1, part))
    operands = arrays + list(after)
    return pl.pallas_call(
        functools.partial(kernel, tuple(views), len(operands)),
        out_shape=out_shape,
        in_specs=[SMEM] * len(scalars) + [VMEM] * len(arrays) + [ANYWHERE] * len(after),
        out_specs=jax.tree.map(lambda _: VMEM, out_shape),
        scratch_shapes=scratch,
        compiler_params=pltpu.CompilerParams(vmem_limit_bytes=limit),
        cost_estimate=pl.CostEstimate(
            flops=int(micros * 1.15e9), bytes_accessed=4 * MIB, transcendentals=0
        ),
    )(*scalars, *operands)


def body(x_band, x_mask, sq_mask, cube_mask):
    high_y = lax.axis_index("row") % 2
    low_y, core = lax.axis_index("col") // 2, lax.axis_index("col") % 2

    own = pl.pallas_call(
        mask_kernel,
        out_shape=jax.ShapeDtypeStruct(x_band.shape, F32),
        in_specs=[SMEM, VMEM],
        out_specs=VMEM,
    )(x_mask, x_band)

    own_m, pair_m = together(send(own, MIRROR), send(own, FLIP))
    both = jnp.stack([own, own_m])
    after = send(both, NEXT)
    pair_o = send(pair_m, MIRROR)
    below, above = send(both, UP), send(both, DOWN)
    twin = send(both, SIBLING)
    beside_m = send(pair_m, ACROSS)
    twin_after = send(after, SIBLING)
    beside_o = send(pair_o, ACROSS)
    far_a = send(pair_o, AGAINST)
    far_b = send(beside_o, ACROSS)

    chips = jnp.stack([low_y, 3 - low_y, low_y ^ 1, (3 - low_y) ^ 1])
    orbitals = jnp.concatenate([2 * chips + core, 2 * chips + 1 - core])
    pair_at, beside_at = 3 - 2 * high_y, 1 + 2 * high_y
    square_rows = jnp.stack([jnp.int32(0), jnp.int32(4), jnp.int32(2), pair_at, beside_at])
    square_places = jnp.concatenate([square_rows, orbitals]).astype(jnp.int32)
    cube_places = [1, 5, 3, pair_at + 1, beside_at + 1, 6 - 6 * high_y, 6 * high_y, low_y, core]
    cube_places = jnp.stack([jnp.int32(v) for v in cube_places])

    left = [(array, part) for array in (both, after, twin, twin_after) for part in (0, 1)]

    def square_of(part, pair, beside, behind):
        return call(
            square_kernel,
            (square_places, sq_mask),
            [(below, part), (above, part), (both, part), pair, beside] + left,
            jax.ShapeDtypeStruct((3, 19, 16, 128), F32),
            [
                pltpu.VMEM((15, 208, 384), BF16),
                pltpu.VMEM((15, 384, 384), BF16),
                pltpu.VMEM((3, 29, 16, 128), F32),
            ],
            20 * MIB,
            4.5,
            behind,
        )

    square_m = square_of(1, pair_m, beside_m, (beside_o,))
    twin_m, next_m = send(square_m, SIBLING), send(square_m, NEXT)
    square_o = square_of(0, pair_o, beside_o, (twin_m, far_a))
    twin_o, next_o = send(square_o, SIBLING), send(square_o, NEXT)
    total, window = call(
        cube_first_kernel,
        (cube_places,),
        [(below, 0), (above, 0), (both, 0), pair_o, beside_o, far_a, far_b]
        + [square_o, square_m, twin_o, twin_m],
        (
            jax.ShapeDtypeStruct((3, 35, 16, 128), F32),
            jax.ShapeDtypeStruct((21, 208, 256), BF16),
        ),
        [pltpu.VMEM((21, 208, 256), BF16), pltpu.VMEM((21, 256, 384), BF16)],
        24 * MIB,
        5,
    )
    return call(
        cube_second_kernel,
        (cube_places, cube_mask),
        [total, window, square_o, next_o, next_m, send(next_o, SIBLING), send(next_m, SIBLING)],
        jax.ShapeDtypeStruct((3, 25, 16, 128), F32),
        [pltpu.VMEM((21, 256, 384), BF16), pltpu.VMEM((3, 35, 16, 128), F32)],
        20 * MIB,
        4,
    )


def solution(mesh):
    return jax.shard_map(
        body,
        mesh=mesh,
        in_specs=(P("row", None, "col", None), P("row", None), P("row", None), P("row", None)),
        out_specs=P("row", None, "col", None),
        check_vma=False,
    )
```

```python
import functools

import jax
import jax.numpy as jnp
from jax import lax
from jax.experimental import pallas as pl
from jax.experimental.pallas import tpu as pltpu
from jax.sharding import PartitionSpec as P

Z, X, YH, YL, CORES = 12, 4, 2, 4, 2
CHAIN = Z * X
AXES = ("row", "col")
F32, BF16 = jnp.float32, jnp.bfloat16


def pairs(target):
    listed = []
    for c in range(CHAIN):
        for yh in range(YH):
            for yl in range(YL):
                for core in range(CORES):
                    to = target(c, yh, yl, core)
                    if to is not None:
                        tc, th, tl, tk = to
                        source = ((c * YH + yh) * YL + yl) * CORES + core
                        listed.append((source, (((tc % CHAIN) * YH + th) * YL + tl) * CORES + tk))
    return listed


UP = pairs(lambda c, h, l, k: (c + 1, h, l, k))
DOWN = pairs(lambda c, h, l, k: (c - 1, h, l, k))
ACROSS = pairs(lambda c, h, l, k: (c + 1 if h == 0 else c - 1, h, l, k))
AGAINST = pairs(lambda c, h, l, k: (c - 1 if h == 0 else c + 1, h, l, k))
FLIP = pairs(lambda c, h, l, k: (c, 1 - h, 3 - l, k))
MIRROR = pairs(lambda c, h, l, k: (c, h, 3 - l, k))
NEXT = pairs(lambda c, h, l, k: (c, h, l ^ 1, k))
SIBLING = pairs(lambda c, h, l, k: (c, h, l, 1 - k))


def send(array, which):
    return lax.ppermute(array, AXES, which)


def together(*arrays):
    return lax.optimization_barrier(arrays)


def split(values):
    high = values.astype(BF16)
    return high, (values - high.astype(F32)).astype(BF16)


def mask_kernel(mask_ref, x_ref, out_ref):
    for g in range(x_ref.shape[0]):
        for d in range(x_ref.shape[1]):
            out_ref[g, d] = x_ref[g, d] * mask_ref[g, d].astype(F32)


def lanes(g):
    return slice(128 * g, 128 * (g + 1))


def blank_corners(right_ref, blocks):
    for g in range(3):
        for r in range(blocks + 2):
            if not 0 <= r - g < blocks:
                right_ref[r, :, lanes(g)] = jnp.zeros((right_ref.shape[1], 128), BF16)


def put_right(right_ref, at, slab):
    blocks = slab.shape[1]
    for g in range(3):
        high, low = split(slab[g])
        for first, is_high in at:
            spot = pl.ds(pl.multiple_of(first, 16), 16)
            right_ref[g : g + blocks, spot, lanes(g)] = high if is_high else low


def accumulate(window_ref, right_ref, total_ref):
    for r in range(window_ref.shape[0]):
        product = jnp.dot(window_ref[r], right_ref[r], preferred_element_type=F32)
        product = product.reshape(13, 16, 384)
        for g in range(3):
            total_ref[g, r + 2 - g : r + 15 - g] += product[:, :, lanes(g)]


def viewed(refs, views):
    return [refs[n] if part is None else refs[n].at[part] for n, part in views]


def square_kernel(views, arrays, place_ref, mask_ref, *refs):
    given = viewed(refs, views)
    rows, slabs = given[:5], given[5:]
    out_ref, window_ref, right_ref, total_ref = refs[arrays:]
    for n, ref in enumerate(rows):
        base = place_ref[n] * 3
        for j in range(3):
            high, low = split(ref[j].reshape(208, 128))
            for part, value in enumerate((high, low, high)):
                window_ref[base + j, :, lanes(part)] = value
    blank_corners(right_ref, 13)
    for n, slab in enumerate(slabs):
        at = place_ref[5 + n] * 16
        put_right(right_ref, ((at, True), (128 + at, True), (256 + at, False)), slab)
    total_ref[...] = jnp.zeros_like(total_ref)
    accumulate(window_ref, right_ref, total_ref)
    for g in range(3):
        for e in range(19):
            out_ref[g, e] = total_ref[g, e + 5] * mask_ref[g, e].astype(F32)


def fill_half(right_ref, chips, slabs, core):
    blank_corners(right_ref, 19)
    zero = jnp.zeros((21, 16, 384), BF16)
    for n, chip in enumerate(chips):
        other = lax.rem(chip + 2, 4)
        for k in range(2):
            right_ref[:, pl.ds(pl.multiple_of(128 + 32 * other + 16 * k, 16), 16), :] = zero
        for k, slab in ((core, slabs[n]), (1 - core, slabs[2 + n])):
            place = 32 * chip + 16 * k
            again = 32 * other + 16 * k
            put_right(right_ref, ((place, True), (again, True), (128 + place, False)), slab)


def cube_first_kernel(views, arrays, place_ref, *refs):
    given = viewed(refs, views)
    rows, slabs = given[:7], given[7:]
    total_ref, next_ref, window_ref, right_ref = refs[arrays:]
    low_y, core = place_ref[7], place_ref[8]
    chip = lax.broadcasted_iota(jnp.int32, (208, 128), 1) // 32
    mine = (chip == low_y) | (chip == 3 - low_y)
    for n, ref in enumerate(rows):
        base = place_ref[n] * 3
        for j in range(3):
            values = ref[j].reshape(208, 128)
            rounded = values.astype(BF16)
            high = rounded.astype(F32)
            low = pltpu.roll(values - high, 64, 1)
            window_ref[base + j, :, lanes(0)] = jnp.where(mine, high, low).astype(BF16)
            window_ref[base + j, :, lanes(1)] = rounded
            next_ref[base + j, :, lanes(0)] = jnp.where(mine, low, high).astype(BF16)
            next_ref[base + j, :, lanes(1)] = rounded
    fill_half(right_ref, (low_y, 3 - low_y), slabs, core)
    total_ref[...] = jnp.zeros_like(total_ref)
    accumulate(window_ref, right_ref, total_ref)


def cube_second_kernel(views, arrays, place_ref, mask_ref, *refs):
    given = viewed(refs, views)
    before_ref, window_ref, own_ref, slabs = given[0], given[1], given[2], given[3:]
    out_ref, right_ref, total_ref = refs[arrays:]
    low_y, core = place_ref[7], place_ref[8]
    fill_half(right_ref, (low_y ^ 1, (3 - low_y) ^ 1), slabs, core)
    total_ref[...] = before_ref[...]
    accumulate(window_ref, right_ref, total_ref)
    for g in range(3):
        for f in range(25):
            value = -2.0 * total_ref[g, f + 5]
            if 3 <= f < 22:
                value = 3.0 * own_ref[g, f - 3] + value
            out_ref[g, f] = value * mask_ref[g, f].astype(F32)


SMEM = pl.BlockSpec(memory_space=pltpu.SMEM)
VMEM = pl.BlockSpec(memory_space=pltpu.VMEM)
ANYWHERE = pl.BlockSpec(memory_space=pl.ANY)
MIB = 1024 * 1024


def call(kernel, scalars, given, out_shape, scratch, limit, micros, after=()):
    arrays, views = [], []
    for item in given:
        array, part = item if isinstance(item, tuple) else (item, None)
        held = [n for n, known in enumerate(arrays) if known is array]
        if not held:
            arrays.append(array)
        views.append((held[0] if held else len(arrays) - 1, part))
    operands = arrays + list(after)
    return pl.pallas_call(
        functools.partial(kernel, tuple(views), len(operands)),
        out_shape=out_shape,
        in_specs=[SMEM] * len(scalars) + [VMEM] * len(arrays) + [ANYWHERE] * len(after),
        out_specs=jax.tree.map(lambda _: VMEM, out_shape),
        scratch_shapes=scratch,
        compiler_params=pltpu.CompilerParams(vmem_limit_bytes=limit),
        cost_estimate=pl.CostEstimate(
            flops=int(micros * 1.15e9), bytes_accessed=4 * MIB, transcendentals=0
        ),
    )(*scalars, *operands)


def body(x_band, x_mask, sq_mask, cube_mask):
    high_y = lax.axis_index("row") % 2
    low_y, core = lax.axis_index("col") // 2, lax.axis_index("col") % 2

    own = pl.pallas_call(
        mask_kernel,
        out_shape=jax.ShapeDtypeStruct(x_band.shape, F32),
        in_specs=[SMEM, VMEM],
        out_specs=VMEM,
    )(x_mask, x_band)

    own_m, pair_m, below_o, above_o = together(
        send(own, MIRROR), send(own, FLIP), send(own, UP), send(own, DOWN)
    )
    both = jnp.stack([own, own_m])
    after, twin = send(both, NEXT), send(both, SIBLING)
    pair_o, below_m, above_m, beside_m = together(
        send(pair_m, MIRROR), send(own_m, UP), send(own_m, DOWN), send(pair_m, ACROSS)
    )
    beside_o, far_a = together(send(pair_o, ACROSS), send(pair_o, AGAINST))
    twin_after = send(after, SIBLING)
    far_b = send(beside_o, ACROSS)

    chips = jnp.stack([low_y, 3 - low_y, low_y ^ 1, (3 - low_y) ^ 1])
    orbitals = jnp.concatenate([2 * chips + core, 2 * chips + 1 - core])
    pair_at, beside_at = 3 - 2 * high_y, 1 + 2 * high_y
    square_rows = jnp.stack([jnp.int32(0), jnp.int32(4), jnp.int32(2), pair_at, beside_at])
    square_places = jnp.concatenate([square_rows, orbitals]).astype(jnp.int32)
    cube_places = [1, 5, 3, pair_at + 1, beside_at + 1, 6 - 6 * high_y, 6 * high_y, low_y, core]
    cube_places = jnp.stack([jnp.int32(v) for v in cube_places])

    left = [(array, part) for array in (both, after, twin, twin_after) for part in (0, 1)]

    def square_of(rows, behind):
        return call(
            square_kernel,
            (square_places, sq_mask),
            rows + left,
            jax.ShapeDtypeStruct((3, 19, 16, 128), F32),
            [
                pltpu.VMEM((15, 208, 384), BF16),
                pltpu.VMEM((15, 384, 384), BF16),
                pltpu.VMEM((3, 29, 16, 128), F32),
            ],
            14 * MIB,
            0.2,
            behind,
        )

    square_m = square_of([below_m, above_m, (both, 1), pair_m, beside_m], (beside_o,))
    twin_m, next_m = send(square_m, SIBLING), send(square_m, NEXT)
    square_o = square_of([below_o, above_o, (both, 0), pair_o, beside_o], (twin_m,))
    twin_o, next_o = send(square_o, SIBLING), send(square_o, NEXT)
    total, window = call(
        cube_first_kernel,
        (cube_places,),
        [below_o, above_o, (both, 0), pair_o, beside_o, far_a, far_b]
        + [square_o, square_m, twin_o, twin_m],
        (
            jax.ShapeDtypeStruct((3, 35, 16, 128), F32),
            jax.ShapeDtypeStruct((21, 208, 256), BF16),
        ),
        [pltpu.VMEM((21, 208, 256), BF16), pltpu.VMEM((21, 256, 384), BF16)],
        17 * MIB,
        5,
    )
    return call(
        cube_second_kernel,
        (cube_places, cube_mask),
        [total, window, square_o, next_o, next_m, send(next_o, SIBLING), send(next_m, SIBLING)],
        jax.ShapeDtypeStruct((3, 25, 16, 128), F32),
        [pltpu.VMEM((21, 256, 384), BF16), pltpu.VMEM((3, 35, 16, 128), F32)],
        14 * MIB,
        4,
    )


def solution(mesh):
    return jax.shard_map(
        body,
        mesh=mesh,
        in_specs=(P("row", None, "col", None), P("row", None), P("row", None), P("row", None)),
        out_specs=P("row", None, "col", None),
        check_vma=False,
    )
```

```python
import functools

import jax
import jax.numpy as jnp
from jax import lax
from jax.experimental import pallas as pl
from jax.experimental.pallas import tpu as pltpu
from jax.sharding import PartitionSpec as P

Z, X, YH, YL, CORES = 12, 4, 2, 4, 2
CHAIN = Z * X
AXES = ("row", "col")
F32, BF16 = jnp.float32, jnp.bfloat16


def pairs(target):
    listed = []
    for c in range(CHAIN):
        for yh in range(YH):
            for yl in range(YL):
                for core in range(CORES):
                    to = target(c, yh, yl, core)
                    if to is not None:
                        tc, th, tl, tk = to
                        source = ((c * YH + yh) * YL + yl) * CORES + core
                        listed.append((source, (((tc % CHAIN) * YH + th) * YL + tl) * CORES + tk))
    return listed


UP = pairs(lambda c, h, l, k: (c + 1, h, l, k))
DOWN = pairs(lambda c, h, l, k: (c - 1, h, l, k))
ACROSS = pairs(lambda c, h, l, k: (c + 1 if h == 0 else c - 1, h, l, k))
AGAINST = pairs(lambda c, h, l, k: (c - 1 if h == 0 else c + 1, h, l, k))
FLIP = pairs(lambda c, h, l, k: (c, 1 - h, 3 - l, k))
MIRROR = pairs(lambda c, h, l, k: (c, h, 3 - l, k))
NEXT = pairs(lambda c, h, l, k: (c, h, l ^ 1, k))
SIBLING = pairs(lambda c, h, l, k: (c, h, l, 1 - k))


def send(array, which):
    return lax.ppermute(array, AXES, which)


def together(*arrays):
    return lax.optimization_barrier(arrays)


def split(values):
    high = values.astype(BF16)
    return high, (values - high.astype(F32)).astype(BF16)


def mask_kernel(mask_ref, x_ref, out_ref):
    for g in range(x_ref.shape[0]):
        for d in range(x_ref.shape[1]):
            out_ref[g, d] = x_ref[g, d] * mask_ref[g, d].astype(F32)


def lanes(g):
    return slice(128 * g, 128 * (g + 1))


def blank_corners(right_ref, blocks):
    for g in range(3):
        for r in range(blocks + 2):
            if not 0 <= r - g < blocks:
                right_ref[r, :, lanes(g)] = jnp.zeros((right_ref.shape[1], 128), BF16)


def put_right(right_ref, at, slab):
    blocks = slab.shape[1]
    for g in range(3):
        high, low = split(slab[g])
        for first, is_high in at:
            spot = pl.ds(pl.multiple_of(first, 16), 16)
            right_ref[g : g + blocks, spot, lanes(g)] = high if is_high else low


def accumulate(window_ref, right_ref, total_ref):
    rows = window_ref.shape[2]
    for r in range(window_ref.shape[0]):
        left = window_ref[r].reshape(13 * rows, window_ref.shape[3])
        product = jnp.dot(left, right_ref[r], preferred_element_type=F32)
        product = product.reshape(13, rows, 384)
        for g in range(3):
            total_ref[g, r + 2 - g : r + 15 - g] += product[:, :, lanes(g)]


def fetched(given, scratch, semaphores):
    copies = [
        pltpu.make_async_copy(ref, held, semaphores.at[n])
        for n, (ref, held) in enumerate(zip(given, scratch))
    ]
    for copy in copies:
        copy.start()

    def arrived(copy, held):
        def wait():
            copy.wait()
            return held

        return wait

    return [arrived(copy, held) for copy, held in zip(copies, scratch)]


def square_kernel(place_ref, mask_ref, given, out_ref, window_ref, right_ref, total_ref):
    rows, slabs = given[:10], given[10:]
    blank_corners(right_ref, 13)
    total_ref[...] = jnp.zeros_like(total_ref)
    for n, wait in enumerate(slabs):
        at = place_ref[5 + n] * 16
        put_right(right_ref, ((at, True), (128 + at, True), (256 + at, False)), wait())
    for n in range(5):
        base = place_ref[n] * 3
        for side in range(2):
            ref = rows[2 * n + side]()
            for j in range(3):
                high, low = split(ref[j])
                for part, value in enumerate((high, low, high)):
                    window_ref[base + j, :, 16 * side : 16 * side + 16, lanes(part)] = value
    accumulate(window_ref, right_ref, total_ref)
    for g in range(3):
        for e in range(19):
            kept = mask_ref[g, e].astype(F32)
            for side in range(2):
                out_ref[side, g, e] = total_ref[g, e + 5, 16 * side : 16 * side + 16] * kept


def fill_half(right_ref, chips, slabs, core):
    blank_corners(right_ref, 19)
    zero = jnp.zeros((21, 16, 384), BF16)
    for n, chip in enumerate(chips):
        other = lax.rem(chip + 2, 4)
        for k in range(2):
            right_ref[:, pl.ds(pl.multiple_of(128 + 32 * other + 16 * k, 16), 16), :] = zero
        for k, slab in ((core, slabs[n]), (1 - core, slabs[2 + n])):
            place = 32 * chip + 16 * k
            again = 32 * other + 16 * k
            put_right(right_ref, ((place, True), (again, True), (128 + place, False)), slab())


def cube_first_kernel(place_ref, given, total_ref, next_ref, window_ref, right_ref):
    rows, slabs = given[:7], given[7:]
    low_y, core = place_ref[7], place_ref[8]
    fill_half(right_ref, (low_y, 3 - low_y), slabs, core)
    chip = lax.broadcasted_iota(jnp.int32, (208, 128), 1) // 32
    mine = (chip == low_y) | (chip == 3 - low_y)
    blocks = window_ref.shape[1:3] + (128,)
    for n, wait in enumerate(rows):
        base = place_ref[n] * 3
        ref = wait()
        for j in range(3):
            values = ref[j].reshape(208, 128)
            rounded = values.astype(BF16)
            high = rounded.astype(F32)
            low = pltpu.roll(values - high, 64, 1)
            first = jnp.where(mine, high, low).astype(BF16)
            second = jnp.where(mine, low, high).astype(BF16)
            window_ref[base + j, :, :, lanes(0)] = first.reshape(blocks)
            window_ref[base + j, :, :, lanes(1)] = rounded.reshape(blocks)
            next_ref[base + j, :, :, lanes(0)] = second.reshape(blocks)
            next_ref[base + j, :, :, lanes(1)] = rounded.reshape(blocks)
    total_ref[...] = jnp.zeros_like(total_ref)
    accumulate(window_ref, right_ref, total_ref)


def cube_second_kernel(place_ref, mask_ref, given, out_ref, right_ref):
    before, window, own, slabs = given[0], given[1], given[2], given[3:]
    low_y, core = place_ref[7], place_ref[8]
    fill_half(right_ref, (low_y ^ 1, (3 - low_y) ^ 1), slabs, core)
    total_ref, window_ref, own_ref = before(), window(), own()
    accumulate(window_ref, right_ref, total_ref)
    for g in range(3):
        for f in range(25):
            value = -2.0 * total_ref[g, f + 5]
            if 3 <= f < 22:
                value = 3.0 * own_ref[g, f - 3] + value
            out_ref[g, f] = value * mask_ref[g, f].astype(F32)


SMEM = pl.BlockSpec(memory_space=pltpu.SMEM)
VMEM = pl.BlockSpec(memory_space=pltpu.VMEM)
IN_HBM = pl.BlockSpec(memory_space=pltpu.HBM)
MIB = 1024 * 1024
LIMIT = 60


def call(kernel, scalars, given, out_shape, scratch, micros):
    arrays, views, held = [], [], []
    for item in given:
        array, part = item if isinstance(item, tuple) else (item, None)
        known = [n for n, other in enumerate(arrays) if other is array]
        if not known:
            arrays.append(array)
        views.append((known[0] if known else len(arrays) - 1, part))
        held.append(pltpu.VMEM(array.shape if part is None else array.shape[1:], array.dtype))
    first = len(scalars)
    last = first + len(arrays)
    outs = len(jax.tree.leaves(out_shape))

    def whole(*refs):
        parts = [refs[first + n] if p is None else refs[first + n].at[p] for n, p in views]
        own, brought = refs[last : len(refs) - len(held) - 1], refs[len(refs) - len(held) - 1 : -1]
        kernel(*refs[:first], fetched(parts, brought, refs[-1]), *own)

    return pl.pallas_call(
        whole,
        out_shape=out_shape,
        in_specs=[SMEM] * first + [IN_HBM] * len(arrays),
        out_specs=jax.tree.map(lambda _: VMEM, out_shape),
        scratch_shapes=scratch + held + [pltpu.SemaphoreType.DMA((len(held),))],
        compiler_params=pltpu.CompilerParams(vmem_limit_bytes=LIMIT * MIB),
        cost_estimate=pl.CostEstimate(
            flops=int(micros * 1.15e9), bytes_accessed=int(micros * MIB), transcendentals=0
        ),
    )(*scalars, *arrays)


def body(x_band, x_mask, sq_mask, cube_mask):
    high_y = lax.axis_index("row") % 2
    low_y, core = lax.axis_index("col") // 2, lax.axis_index("col") % 2

    own = pl.pallas_call(
        mask_kernel,
        out_shape=jax.ShapeDtypeStruct(x_band.shape, F32),
        in_specs=[SMEM, VMEM],
        out_specs=VMEM,
    )(x_mask, x_band)

    own_m, pair_m, below_o, above_o = together(
        send(own, MIRROR), send(own, FLIP), send(own, UP), send(own, DOWN)
    )
    both = jnp.stack([own, own_m])
    after, twin = send(both, NEXT), send(both, SIBLING)
    pair_o, below_m, above_m = together(
        send(pair_m, MIRROR), send(own_m, UP), send(own_m, DOWN)
    )
    pair = jnp.stack([pair_o, pair_m])
    beside, twin_after = send(pair, ACROSS), send(after, SIBLING)

    chips = jnp.stack([low_y, 3 - low_y, low_y ^ 1, (3 - low_y) ^ 1])
    orbitals = jnp.concatenate([2 * chips + core, 2 * chips + 1 - core])
    pair_at, beside_at = 3 - 2 * high_y, 1 + 2 * high_y
    square_rows = jnp.stack([jnp.int32(0), jnp.int32(4), jnp.int32(2), pair_at, beside_at])
    square_places = jnp.concatenate([square_rows, orbitals]).astype(jnp.int32)
    cube_places = [1, 5, 3, pair_at + 1, beside_at + 1, 6 - 6 * high_y, 6 * high_y, low_y, core]
    cube_places = jnp.stack([jnp.int32(v) for v in cube_places])

    left = [(array, part) for array in (both, after, twin, twin_after) for part in (0, 1)]

    square = call(
        square_kernel,
        (square_places, sq_mask),
        [below_o, below_m, above_o, above_m, (both, 0), (both, 1)]
        + [(pair, 0), (pair, 1), (beside, 0), (beside, 1)]
        + left,
        jax.ShapeDtypeStruct((2, 3, 19, 16, 128), F32),
        [
            pltpu.VMEM((15, 13, 32, 384), BF16),
            pltpu.VMEM((15, 384, 384), BF16),
            pltpu.VMEM((3, 29, 32, 128), F32),
        ],
        0.01,
    )
    square_after = send(square, NEXT)
    square_twin, pair_late, beside_late = together(send(square, SIBLING), pair_o, beside)
    far_a, far_b = send(pair_late, AGAINST), send(beside_late, ACROSS)
    total, window = call(
        cube_first_kernel,
        (cube_places,),
        [below_o, above_o, (both, 0), (pair, 0), (beside, 0), far_a, (far_b, 0)]
        + [(square, 0), (square, 1), (square_twin, 0), (square_twin, 1)],
        (
            jax.ShapeDtypeStruct((3, 35, 16, 128), F32),
            jax.ShapeDtypeStruct((21, 13, 16, 256), BF16),
        ),
        [pltpu.VMEM((21, 13, 16, 256), BF16), pltpu.VMEM((21, 256, 384), BF16)],
        0.01,
    )
    total, square_after = together(total, square_after)
    after_twin = send(square_after, SIBLING)
    return call(
        cube_second_kernel,
        (cube_places, cube_mask),
        [total, window, (square, 0), (square_after, 0), (square_after, 1)]
        + [(after_twin, 0), (after_twin, 1)],
        jax.ShapeDtypeStruct((3, 25, 16, 128), F32),
        [pltpu.VMEM((21, 256, 384), BF16)],
        4,
    )


def solution(mesh):
    return jax.shard_map(
        body,
        mesh=mesh,
        in_specs=(P("row", None, "col", None), P("row", None), P("row", None), P("row", None)),
        out_specs=P("row", None, "col", None),
        check_vma=False,
    )
```

```python
import functools

import jax
import jax.numpy as jnp
from jax import lax
from jax.experimental import pallas as pl
from jax.experimental.pallas import tpu as pltpu
from jax.sharding import PartitionSpec as P

Z, X, YH, YL, CORES = 12, 4, 2, 4, 2
CHAIN = Z * X
AXES = ("row", "col")
F32, BF16 = jnp.float32, jnp.bfloat16


def pairs(target):
    listed = []
    for c in range(CHAIN):
        for yh in range(YH):
            for yl in range(YL):
                for core in range(CORES):
                    to = target(c, yh, yl, core)
                    if to is not None:
                        tc, th, tl, tk = to
                        source = ((c * YH + yh) * YL + yl) * CORES + core
                        listed.append((source, (((tc % CHAIN) * YH + th) * YL + tl) * CORES + tk))
    return listed


UP = pairs(lambda c, h, l, k: (c + 1, h, l, k))
DOWN = pairs(lambda c, h, l, k: (c - 1, h, l, k))
ACROSS = pairs(lambda c, h, l, k: (c + 1 if h == 0 else c - 1, h, l, k))
AGAINST = pairs(lambda c, h, l, k: (c - 1 if h == 0 else c + 1, h, l, k))
FLIP = pairs(lambda c, h, l, k: (c, 1 - h, 3 - l, k))
MIRROR = pairs(lambda c, h, l, k: (c, h, 3 - l, k))
NEXT = pairs(lambda c, h, l, k: (c, h, l ^ 1, k))
SIBLING = pairs(lambda c, h, l, k: (c, h, l, 1 - k))


def send(array, which):
    return lax.ppermute(array, AXES, which)


def together(*arrays):
    return lax.optimization_barrier(arrays)


def split(values):
    high = values.astype(BF16)
    return high, (values - high.astype(F32)).astype(BF16)


def mask_kernel(mask_ref, x_ref, out_ref):
    for g in range(x_ref.shape[0]):
        for d in range(x_ref.shape[1]):
            out_ref[g, d] = x_ref[g, d] * mask_ref[g, d].astype(F32)


def lanes(g):
    return slice(128 * g, 128 * (g + 1))


def blank_corners(right_ref, blocks):
    for g in range(3):
        for r in range(blocks + 2):
            if not 0 <= r - g < blocks:
                right_ref[r, :, lanes(g)] = jnp.zeros((right_ref.shape[1], 128), BF16)


def put_right(right_ref, at, slab):
    blocks = slab.shape[1]
    for g in range(3):
        high, low = split(slab[g])
        for first, is_high in at:
            spot = pl.ds(pl.multiple_of(first, 16), 16)
            right_ref[g : g + blocks, spot, lanes(g)] = high if is_high else low


def accumulate(pieces, total_ref, rows, firsts):
    for (left, right), r in zip(pieces, firsts):
        product = jnp.dot(left, right, preferred_element_type=F32).reshape(13, rows, 384)
        for g in range(3):
            total_ref[g, pl.ds(r + 2 - g, 13)] += product[:, :, lanes(g)]


def all_rows(window_ref, right_ref, total_ref):
    count, _, rows, depth = window_ref.shape
    pieces = ((window_ref[r].reshape(13 * rows, depth), right_ref[r]) for r in range(count))
    accumulate(pieces, total_ref, rows, range(count))


def fetched(given, scratch, semaphores):
    copies = [
        pltpu.make_async_copy(ref, held, semaphores.at[n])
        for n, (ref, held) in enumerate(zip(given, scratch))
    ]
    for copy in copies:
        copy.start()

    def arrived(copy, held):
        def wait():
            copy.wait()
            return held

        return wait

    return [arrived(copy, held) for copy, held in zip(copies, scratch)]


def here(ref):
    return lambda: ref


def put_left(window_ref, base, side, ref):
    for j in range(3):
        high, low = split(ref[j])
        for part, value in enumerate((high, low, high)):
            window_ref[base + j, :, 16 * side : 16 * side + 16, lanes(part)] = value


def square_first_kernel(
    place_ref, given, total_ref, rest_ref, window_ref, right_ref
):
    rows, slabs = given[:8], given[8:]
    blank_corners(right_ref, 13)
    total_ref[...] = jnp.zeros_like(total_ref)
    for n, wait in enumerate(slabs):
        at = place_ref[5 + n] * 16
        put_right(right_ref, ((at, True), (128 + at, True), (256 + at, False)), wait())
    for n in range(4):
        for side in range(2):
            put_left(window_ref, 3 * n, side, rows[2 * n + side]())
    for j in range(3):
        rest_ref[j] = right_ref[place_ref[4] * 3 + j]
    firsts = [place_ref[n] * 3 + j for n in range(4) for j in range(3)]
    pieces = (
        (window_ref[n].reshape(13 * 32, 384), right_ref[r]) for n, r in enumerate(firsts)
    )
    accumulate(pieces, total_ref, 32, firsts)


def square_second_kernel(place_ref, mask_ref, given, out_ref, sent_ref, window_ref):
    before, rest, beside_o, beside_m = given
    kept_o = beside_o()
    put_left(window_ref, 0, 0, kept_o)
    put_left(window_ref, 0, 1, beside_m())
    sent_ref[...] = kept_o[...]
    total_ref, right_ref = before(), rest()
    firsts = [place_ref[4] * 3 + j for j in range(3)]
    pieces = ((window_ref[j].reshape(13 * 32, 384), right_ref[j]) for j in range(3))
    accumulate(pieces, total_ref, 32, firsts)
    for g in range(3):
        for e in range(19):
            kept = mask_ref[g, e].astype(F32)
            for side in range(2):
                out_ref[side, g, e] = total_ref[g, e + 5, 16 * side : 16 * side + 16] * kept


def fill_half(right_ref, chips, slabs, core):
    blank_corners(right_ref, 19)
    zero = jnp.zeros((21, 16, 384), BF16)
    for n, chip in enumerate(chips):
        other = lax.rem(chip + 2, 4)
        for k in range(2):
            right_ref[:, pl.ds(pl.multiple_of(128 + 32 * other + 16 * k, 16), 16), :] = zero
        for k, slab in ((core, slabs[n]), (1 - core, slabs[2 + n])):
            place = 32 * chip + 16 * k
            again = 32 * other + 16 * k
            put_right(right_ref, ((place, True), (again, True), (128 + place, False)), slab())


def cube_first_kernel(place_ref, given, total_ref, next_ref, window_ref, right_ref):
    rows, slabs = given[:7], given[7:]
    low_y, core = place_ref[7], place_ref[8]
    fill_half(right_ref, (low_y, 3 - low_y), slabs, core)
    chip = lax.broadcasted_iota(jnp.int32, (208, 128), 1) // 32
    mine = (chip == low_y) | (chip == 3 - low_y)
    blocks = window_ref.shape[1:3] + (128,)
    for n, wait in enumerate(rows):
        base = place_ref[n] * 3
        ref = wait()
        for j in range(3):
            values = ref[j].reshape(208, 128)
            rounded = values.astype(BF16)
            high = rounded.astype(F32)
            low = pltpu.roll(values - high, 64, 1)
            first = jnp.where(mine, high, low).astype(BF16)
            second = jnp.where(mine, low, high).astype(BF16)
            window_ref[base + j, :, :, lanes(0)] = first.reshape(blocks)
            window_ref[base + j, :, :, lanes(1)] = rounded.reshape(blocks)
            next_ref[base + j, :, :, lanes(0)] = second.reshape(blocks)
            next_ref[base + j, :, :, lanes(1)] = rounded.reshape(blocks)
    total_ref[...] = jnp.zeros_like(total_ref)
    all_rows(window_ref, right_ref, total_ref)


def cube_second_kernel(place_ref, mask_ref, given, out_ref, right_ref, total_ref):
    before, window, own, slabs = given[0], given[1], given[2], given[3:]
    low_y, core = place_ref[7], place_ref[8]
    fill_half(right_ref, (low_y ^ 1, (3 - low_y) ^ 1), slabs, core)
    total_ref[...] = before()[...]
    window_ref, own_ref = window(), own()
    all_rows(window_ref, right_ref, total_ref)
    for g in range(3):
        for f in range(25):
            value = -2.0 * total_ref[g, f + 5]
            if 3 <= f < 22:
                value = 3.0 * own_ref[g, f - 3] + value
            out_ref[g, f] = value * mask_ref[g, f].astype(F32)


SMEM = pl.BlockSpec(memory_space=pltpu.SMEM)
VMEM = pl.BlockSpec(memory_space=pltpu.VMEM)
IN_HBM = pl.BlockSpec(memory_space=pltpu.HBM)
MIB = 1024 * 1024
LARGE, SMALL = 60, 24


def call(kernel, scalars, given, out_shape, scratch, limit, fetch):
    arrays, views, held = [], [], []
    for item in given:
        array, part = item if isinstance(item, tuple) else (item, None)
        known = [n for n, other in enumerate(arrays) if other is array]
        if not known:
            arrays.append(array)
        views.append((known[0] if known else len(arrays) - 1, part))
        held.append(pltpu.VMEM(array.shape if part is None else array.shape[1:], array.dtype))
    first = len(scalars)
    last = first + len(arrays)
    extra = held + [pltpu.SemaphoreType.DMA((len(held),))] if fetch else []

    def whole(*refs):
        parts = [refs[first + n] if p is None else refs[first + n].at[p] for n, p in views]
        end = len(refs) - len(extra)
        waits = fetched(parts, refs[end:-1], refs[-1]) if fetch else [here(p) for p in parts]
        kernel(*refs[:first], waits, *refs[last:end])

    return pl.pallas_call(
        whole,
        out_shape=out_shape,
        in_specs=[SMEM] * first + [IN_HBM if fetch else VMEM] * len(arrays),
        out_specs=jax.tree.map(lambda _: VMEM, out_shape),
        scratch_shapes=scratch + extra,
        compiler_params=pltpu.CompilerParams(vmem_limit_bytes=limit * MIB),
        cost_estimate=pl.CostEstimate(flops=1000000, bytes_accessed=1000, transcendentals=0),
    )(*scalars, *arrays)


def body(x_band, x_mask, sq_mask, cube_mask):
    high_y = lax.axis_index("row") % 2
    low_y, core = lax.axis_index("col") // 2, lax.axis_index("col") % 2

    own = pl.pallas_call(
        mask_kernel,
        out_shape=jax.ShapeDtypeStruct(x_band.shape, F32),
        in_specs=[SMEM, VMEM],
        out_specs=VMEM,
    )(x_mask, x_band)

    own_m, pair_m, below_o, above_o = together(
        send(own, MIRROR), send(own, FLIP), send(own, UP), send(own, DOWN)
    )
    both = jnp.stack([own, own_m])
    after, twin = send(both, NEXT), send(both, SIBLING)
    pair_o = send(pair_m, MIRROR)
    after, below_m, above_m = together(after, send(own_m, UP), send(own_m, DOWN))
    pair = jnp.stack([pair_o, pair_m])
    beside, twin_after = send(pair, ACROSS), send(after, SIBLING)

    chips = jnp.stack([low_y, 3 - low_y, low_y ^ 1, (3 - low_y) ^ 1])
    orbitals = jnp.concatenate([2 * chips + core, 2 * chips + 1 - core])
    pair_at, beside_at = 3 - 2 * high_y, 1 + 2 * high_y
    square_rows = jnp.stack([jnp.int32(0), jnp.int32(4), jnp.int32(2), pair_at, beside_at])
    square_places = jnp.concatenate([square_rows, orbitals]).astype(jnp.int32)
    cube_places = [1, 5, 3, pair_at + 1, beside_at + 1, 6 - 6 * high_y, 6 * high_y, low_y, core]
    cube_places = jnp.stack([jnp.int32(v) for v in cube_places])

    left = [(array, part) for array in (both, after, twin, twin_after) for part in (0, 1)]

    partial, rest = call(
        square_first_kernel,
        (square_places,),
        [below_o, below_m, above_o, above_m, (both, 0), (both, 1), (pair, 0), (pair, 1)] + left,
        (
            jax.ShapeDtypeStruct((3, 29, 32, 128), F32),
            jax.ShapeDtypeStruct((3, 384, 384), BF16),
        ),
        [pltpu.VMEM((12, 13, 32, 384), BF16), pltpu.VMEM((15, 384, 384), BF16)],
        LARGE,
        True,
    )
    square, beside_o = call(
        square_second_kernel,
        (square_places, sq_mask),
        [partial, rest, (beside, 0), (beside, 1)],
        (
            jax.ShapeDtypeStruct((2, 3, 19, 16, 128), F32),
            jax.ShapeDtypeStruct((3, 13, 16, 128), F32),
        ),
        [pltpu.VMEM((3, 13, 32, 384), BF16)],
        LARGE,
        True,
    )
    square_after = send(square, NEXT)
    square_twin, pair_late, beside_late = together(send(square, SIBLING), pair_o, beside_o)
    far_a, far_b = send(pair_late, AGAINST), send(beside_late, ACROSS)
    total, window = call(
        cube_first_kernel,
        (cube_places,),
        [below_o, above_o, (both, 0), (pair, 0), beside_o, far_a, far_b]
        + [(square, 0), (square, 1), (square_twin, 0), (square_twin, 1)],
        (
            jax.ShapeDtypeStruct((3, 35, 16, 128), F32),
            jax.ShapeDtypeStruct((21, 13, 16, 256), BF16),
        ),
        [pltpu.VMEM((21, 13, 16, 256), BF16), pltpu.VMEM((21, 256, 384), BF16)],
        SMALL,
        False,
    )
    total, square_after = together(total, square_after)
    after_twin = send(square_after, SIBLING)
    return call(
        cube_second_kernel,
        (cube_places, cube_mask),
        [total, window, (square, 0), (square_after, 0), (square_after, 1)]
        + [(after_twin, 0), (after_twin, 1)],
        jax.ShapeDtypeStruct((3, 25, 16, 128), F32),
        [pltpu.VMEM((21, 256, 384), BF16), pltpu.VMEM((3, 35, 16, 128), F32)],
        SMALL,
        False,
    )


def solution(mesh):
    return jax.shard_map(
        body,
        mesh=mesh,
        in_specs=(P("row", None, "col", None), P("row", None), P("row", None), P("row", None)),
        out_specs=P("row", None, "col", None),
        check_vma=False,
    )
```

```python
import functools

import jax
import jax.numpy as jnp
from jax import lax
from jax.experimental import pallas as pl
from jax.experimental.pallas import tpu as pltpu
from jax.sharding import PartitionSpec as P

Z, X, YH, YL, CORES = 12, 4, 2, 4, 2
CHAIN = Z * X
AXES = ("row", "col")
F32, BF16 = jnp.float32, jnp.bfloat16


def pairs(target):
    listed = []
    for c in range(CHAIN):
        for yh in range(YH):
            for yl in range(YL):
                for core in range(CORES):
                    to = target(c, yh, yl, core)
                    if to is not None:
                        tc, th, tl, tk = to
                        source = ((c * YH + yh) * YL + yl) * CORES + core
                        listed.append((source, (((tc % CHAIN) * YH + th) * YL + tl) * CORES + tk))
    return listed


UP = pairs(lambda c, h, l, k: (c + 1, h, l, k))
DOWN = pairs(lambda c, h, l, k: (c - 1, h, l, k))
ACROSS = pairs(lambda c, h, l, k: (c + 1 if h == 0 else c - 1, h, l, k))
AGAINST = pairs(lambda c, h, l, k: (c - 1 if h == 0 else c + 1, h, l, k))
FLIP = pairs(lambda c, h, l, k: (c, 1 - h, 3 - l, k))
MIRROR = pairs(lambda c, h, l, k: (c, h, 3 - l, k))
NEXT = pairs(lambda c, h, l, k: (c, h, l ^ 1, k))
SIBLING = pairs(lambda c, h, l, k: (c, h, l, 1 - k))


def send(array, which):
    return lax.ppermute(array, AXES, which)


def together(*arrays):
    return lax.optimization_barrier(arrays)


def split(values):
    high = values.astype(BF16)
    return high, (values - high.astype(F32)).astype(BF16)


def mask_kernel(mask_ref, x_ref, out_ref):
    for g in range(x_ref.shape[0]):
        for d in range(x_ref.shape[1]):
            out_ref[g, d] = x_ref[g, d] * mask_ref[g, d].astype(F32)


def lanes(g):
    return slice(128 * g, 128 * (g + 1))


def blank_corners(right_ref, blocks):
    for g in range(3):
        for r in range(blocks + 2):
            if not 0 <= r - g < blocks:
                right_ref[r, :, lanes(g)] = jnp.zeros((right_ref.shape[1], 128), BF16)


def put_right(right_ref, at, slab):
    blocks = slab.shape[1]
    for g in range(3):
        high, low = split(slab[g])
        for first, is_high in at:
            spot = pl.ds(pl.multiple_of(first, 16), 16)
            right_ref[g : g + blocks, spot, lanes(g)] = high if is_high else low


def accumulate(pieces, total_ref, rows, firsts):
    for (left, right), r in zip(pieces, firsts):
        product = jnp.dot(left, right, preferred_element_type=F32).reshape(13, rows, 384)
        for g in range(3):
            total_ref[g, pl.ds(r + 2 - g, 13)] += product[:, :, lanes(g)]


def all_rows(window_ref, right_ref, total_ref):
    count, _, rows, depth = window_ref.shape
    pieces = ((window_ref[r].reshape(13 * rows, depth), right_ref[r]) for r in range(count))
    accumulate(pieces, total_ref, rows, range(count))


def fetched(given, scratch, semaphores):
    copies = [
        pltpu.make_async_copy(ref, held, semaphores.at[n])
        for n, (ref, held) in enumerate(zip(given, scratch))
    ]
    for copy in copies:
        copy.start()

    def arrived(copy, held):
        def wait():
            copy.wait()
            return held

        return wait

    return [arrived(copy, held) for copy, held in zip(copies, scratch)]


def here(ref):
    return lambda: ref


def put_left(window_ref, base, side, ref):
    for j in range(3):
        high, low = split(ref[j])
        for part, value in enumerate((high, low, high)):
            window_ref[base + j, :, 16 * side : 16 * side + 16, lanes(part)] = value


def square_first_kernel(
    place_ref, given, total_ref, rest_ref, window_ref, right_ref
):
    rows, slabs = given[:8], given[8:]
    blank_corners(right_ref, 13)
    total_ref[...] = jnp.zeros_like(total_ref)
    for n, wait in enumerate(slabs):
        at = place_ref[5 + n] * 16
        put_right(right_ref, ((at, True), (128 + at, True), (256 + at, False)), wait())
    for n in range(4):
        for side in range(2):
            put_left(window_ref, 3 * n, side, rows[2 * n + side]())
    for j in range(3):
        rest_ref[j] = right_ref[place_ref[4] * 3 + j]
    firsts = [place_ref[n] * 3 + j for n in range(4) for j in range(3)]
    pieces = (
        (window_ref[n].reshape(13 * 32, 384), right_ref[r]) for n, r in enumerate(firsts)
    )
    accumulate(pieces, total_ref, 32, firsts)


def square_second_kernel(place_ref, mask_ref, given, out_ref, sent_ref, window_ref):
    before, rest, beside_o, beside_m = given
    kept_o = beside_o()
    put_left(window_ref, 0, 0, kept_o)
    put_left(window_ref, 0, 1, beside_m())
    sent_ref[...] = kept_o[...]
    total_ref, right_ref = before(), rest()
    firsts = [place_ref[4] * 3 + j for j in range(3)]
    pieces = ((window_ref[j].reshape(13 * 32, 384), right_ref[j]) for j in range(3))
    accumulate(pieces, total_ref, 32, firsts)
    for g in range(3):
        for e in range(19):
            kept = mask_ref[g, e].astype(F32)
            for side in range(2):
                out_ref[side, g, e] = total_ref[g, e + 5, 16 * side : 16 * side + 16] * kept


def fill_half(right_ref, chips, slabs, core):
    blank_corners(right_ref, 19)
    zero = jnp.zeros((21, 16, 384), BF16)
    for n, chip in enumerate(chips):
        other = lax.rem(chip + 2, 4)
        for k in range(2):
            right_ref[:, pl.ds(pl.multiple_of(128 + 32 * other + 16 * k, 16), 16), :] = zero
        for k, slab in ((core, slabs[n]), (1 - core, slabs[2 + n])):
            place = 32 * chip + 16 * k
            again = 32 * other + 16 * k
            put_right(right_ref, ((place, True), (again, True), (128 + place, False)), slab())


def cube_first_kernel(place_ref, given, total_ref, next_ref, window_ref, right_ref):
    rows, slabs = given[:7], given[7:]
    low_y, core = place_ref[7], place_ref[8]
    fill_half(right_ref, (low_y, 3 - low_y), slabs, core)
    chip = lax.broadcasted_iota(jnp.int32, (208, 128), 1) // 32
    mine = (chip == low_y) | (chip == 3 - low_y)
    blocks = window_ref.shape[1:3] + (128,)
    for n, wait in enumerate(rows):
        base = place_ref[n] * 3
        ref = wait()
        for j in range(3):
            values = ref[j].reshape(208, 128)
            rounded = values.astype(BF16)
            high = rounded.astype(F32)
            low = pltpu.roll(values - high, 64, 1)
            first = jnp.where(mine, high, low).astype(BF16)
            second = jnp.where(mine, low, high).astype(BF16)
            window_ref[base + j, :, :, lanes(0)] = first.reshape(blocks)
            window_ref[base + j, :, :, lanes(1)] = rounded.reshape(blocks)
            next_ref[base + j, :, :, lanes(0)] = second.reshape(blocks)
            next_ref[base + j, :, :, lanes(1)] = rounded.reshape(blocks)
    total_ref[...] = jnp.zeros_like(total_ref)
    all_rows(window_ref, right_ref, total_ref)


def cube_second_kernel(place_ref, mask_ref, given, out_ref, right_ref, total_ref):
    before, window, own, slabs = given[0], given[1], given[2], given[3:]
    low_y, core = place_ref[7], place_ref[8]
    fill_half(right_ref, (low_y ^ 1, (3 - low_y) ^ 1), slabs, core)
    total_ref[...] = before()[...]
    window_ref, own_ref = window(), own()
    all_rows(window_ref, right_ref, total_ref)
    for g in range(3):
        for f in range(25):
            value = -2.0 * total_ref[g, f + 5]
            if 3 <= f < 22:
                value = 3.0 * own_ref[g, f - 3] + value
            out_ref[g, f] = value * mask_ref[g, f].astype(F32)


SMEM = pl.BlockSpec(memory_space=pltpu.SMEM)
VMEM = pl.BlockSpec(memory_space=pltpu.VMEM)
IN_HBM = pl.BlockSpec(memory_space=pltpu.HBM)
MIB = 1024 * 1024
LARGE, SMALL = 60, 24


def call(kernel, scalars, given, out_shape, scratch, limit, fetch):
    arrays, views, held = [], [], []
    for item in given:
        array, part = item if isinstance(item, tuple) else (item, None)
        known = [n for n, other in enumerate(arrays) if other is array]
        if not known:
            arrays.append(array)
        views.append((known[0] if known else len(arrays) - 1, part))
        held.append(pltpu.VMEM(array.shape if part is None else array.shape[1:], array.dtype))
    first = len(scalars)
    last = first + len(arrays)
    extra = held + [pltpu.SemaphoreType.DMA((len(held),))] if fetch else []

    def whole(*refs):
        parts = [refs[first + n] if p is None else refs[first + n].at[p] for n, p in views]
        end = len(refs) - len(extra)
        waits = fetched(parts, refs[end:-1], refs[-1]) if fetch else [here(p) for p in parts]
        kernel(*refs[:first], waits, *refs[last:end])

    return pl.pallas_call(
        whole,
        out_shape=out_shape,
        in_specs=[SMEM] * first + [IN_HBM if fetch else VMEM] * len(arrays),
        out_specs=jax.tree.map(lambda _: VMEM, out_shape),
        scratch_shapes=scratch + extra,
        compiler_params=pltpu.CompilerParams(vmem_limit_bytes=limit * MIB),
        cost_estimate=pl.CostEstimate(flops=1000000, bytes_accessed=1000, transcendentals=0),
    )(*scalars, *arrays)


def body(x_band, x_mask, sq_mask, cube_mask):
    high_y = lax.axis_index("row") % 2
    low_y, core = lax.axis_index("col") // 2, lax.axis_index("col") % 2

    own = pl.pallas_call(
        mask_kernel,
        out_shape=jax.ShapeDtypeStruct(x_band.shape, F32),
        in_specs=[SMEM, VMEM],
        out_specs=VMEM,
    )(x_mask, x_band)

    own_m, pair_m, below_o, above_o = together(
        send(own, MIRROR), send(own, FLIP), send(own, UP), send(own, DOWN)
    )
    both = jnp.stack([own, own_m])
    pair_o = send(own_m, FLIP)
    after, twin = send(both, NEXT), send(both, SIBLING)
    pair_o, below_m, above_m, beside_m = together(
        pair_o, send(own_m, UP), send(own_m, DOWN), send(pair_m, ACROSS)
    )
    beside_o, twin_after = send(pair_o, ACROSS), send(after, SIBLING)

    chips = jnp.stack([low_y, 3 - low_y, low_y ^ 1, (3 - low_y) ^ 1])
    orbitals = jnp.concatenate([2 * chips + core, 2 * chips + 1 - core])
    pair_at, beside_at = 3 - 2 * high_y, 1 + 2 * high_y
    square_rows = jnp.stack([jnp.int32(0), jnp.int32(4), jnp.int32(2), pair_at, beside_at])
    square_places = jnp.concatenate([square_rows, orbitals]).astype(jnp.int32)
    cube_places = [1, 5, 3, pair_at + 1, beside_at + 1, 6 - 6 * high_y, 6 * high_y, low_y, core]
    cube_places = jnp.stack([jnp.int32(v) for v in cube_places])

    left = [(array, part) for array in (both, after, twin, twin_after) for part in (0, 1)]

    partial, rest = call(
        square_first_kernel,
        (square_places,),
        [below_o, below_m, above_o, above_m, (both, 0), (both, 1), pair_o, pair_m] + left,
        (
            jax.ShapeDtypeStruct((3, 29, 32, 128), F32),
            jax.ShapeDtypeStruct((3, 384, 384), BF16),
        ),
        [pltpu.VMEM((12, 13, 32, 384), BF16), pltpu.VMEM((15, 384, 384), BF16)],
        LARGE,
        True,
    )
    square, beside_late = call(
        square_second_kernel,
        (square_places, sq_mask),
        [partial, rest, beside_o, beside_m],
        (
            jax.ShapeDtypeStruct((2, 3, 19, 16, 128), F32),
            jax.ShapeDtypeStruct((3, 13, 16, 128), F32),
        ),
        [pltpu.VMEM((3, 13, 32, 384), BF16)],
        LARGE,
        True,
    )
    square_after = send(square, NEXT)
    square_twin, pair_late, beside_late = together(send(square, SIBLING), pair_o, beside_o)
    far_a, far_b = send(pair_late, AGAINST), send(beside_late, ACROSS)
    total, window = call(
        cube_first_kernel,
        (cube_places,),
        [below_o, above_o, (both, 0), pair_o, beside_o, far_a, far_b]
        + [(square, 0), (square, 1), (square_twin, 0), (square_twin, 1)],
        (
            jax.ShapeDtypeStruct((3, 35, 16, 128), F32),
            jax.ShapeDtypeStruct((21, 13, 16, 256), BF16),
        ),
        [pltpu.VMEM((21, 13, 16, 256), BF16), pltpu.VMEM((21, 256, 384), BF16)],
        SMALL,
        False,
    )
    total, square_after = together(total, square_after)
    after_twin = send(square_after, SIBLING)
    return call(
        cube_second_kernel,
        (cube_places, cube_mask),
        [total, window, (square, 0), (square_after, 0), (square_after, 1)]
        + [(after_twin, 0), (after_twin, 1)],
        jax.ShapeDtypeStruct((3, 25, 16, 128), F32),
        [pltpu.VMEM((21, 256, 384), BF16), pltpu.VMEM((3, 35, 16, 128), F32)],
        SMALL,
        False,
    )


def solution(mesh):
    return jax.shard_map(
        body,
        mesh=mesh,
        in_specs=(P("row", None, "col", None), P("row", None), P("row", None), P("row", None)),
        out_specs=P("row", None, "col", None),
        check_vma=False,
    )
```

```python
import functools

import jax
import jax.numpy as jnp
from jax import lax
from jax.experimental import pallas as pl
from jax.experimental.pallas import tpu as pltpu
from jax.sharding import PartitionSpec as P

Z, X, YH, YL, CORES = 12, 4, 2, 4, 2
CHAIN = Z * X
AXES = ("row", "col")
F32, BF16 = jnp.float32, jnp.bfloat16


def pairs(target):
    listed = []
    for c in range(CHAIN):
        for yh in range(YH):
            for yl in range(YL):
                for core in range(CORES):
                    to = target(c, yh, yl, core)
                    if to is not None:
                        tc, th, tl, tk = to
                        source = ((c * YH + yh) * YL + yl) * CORES + core
                        listed.append((source, (((tc % CHAIN) * YH + th) * YL + tl) * CORES + tk))
    return listed


UP = pairs(lambda c, h, l, k: (c + 1, h, l, k))
DOWN = pairs(lambda c, h, l, k: (c - 1, h, l, k))
ACROSS = pairs(lambda c, h, l, k: (c + 1 if h == 0 else c - 1, h, l, k))
AGAINST = pairs(lambda c, h, l, k: (c - 1 if h == 0 else c + 1, h, l, k))
FLIP = pairs(lambda c, h, l, k: (c, 1 - h, 3 - l, k))
MIRROR = pairs(lambda c, h, l, k: (c, h, 3 - l, k))
NEXT = pairs(lambda c, h, l, k: (c, h, l ^ 1, k))
SIBLING = pairs(lambda c, h, l, k: (c, h, l, 1 - k))


def send(array, which):
    return lax.ppermute(array, AXES, which)


def together(*arrays):
    return lax.optimization_barrier(arrays)


def split(values):
    high = values.astype(BF16)
    return high, (values - high.astype(F32)).astype(BF16)


def mask_kernel(mask_ref, x_ref, out_ref):
    for g in range(x_ref.shape[0]):
        for d in range(x_ref.shape[1]):
            out_ref[g, d] = x_ref[g, d] * mask_ref[g, d].astype(F32)


def lanes(g):
    return slice(128 * g, 128 * (g + 1))


def blank_corners(right_ref, blocks):
    for g in range(3):
        for r in range(blocks + 2):
            if not 0 <= r - g < blocks:
                right_ref[r, :, lanes(g)] = jnp.zeros((right_ref.shape[1], 128), BF16)


def put_right(right_ref, at, slab):
    blocks = slab.shape[1]
    for g in range(3):
        high, low = split(slab[g])
        for first, is_high in at:
            spot = pl.ds(pl.multiple_of(first, 16), 16)
            right_ref[g : g + blocks, spot, lanes(g)] = high if is_high else low


def add_row(left, right, total_ref, r, strip):
    rows = strip.stop - strip.start
    product = jnp.dot(left, right, preferred_element_type=F32).reshape(13, rows, 384)
    for g in range(3):
        total_ref[g, pl.ds(r + 2 - g, 13), strip] += product[:, :, lanes(g)]


def all_rows(window_ref, right_ref, total_ref):
    count, _, rows, depth = window_ref.shape
    for r in range(count):
        left = window_ref[r].reshape(13 * rows, depth)
        add_row(left, right_ref[r], total_ref, r, slice(0, rows))


def fetched(given, scratch, semaphores):
    copies = [
        pltpu.make_async_copy(ref, held, semaphores.at[n])
        for n, (ref, held) in enumerate(zip(given, scratch))
    ]
    for copy in copies:
        copy.start()

    def arrived(copy, held):
        def wait():
            copy.wait()
            return held

        return wait

    return [arrived(copy, held) for copy, held in zip(copies, scratch)]


def here(ref):
    return lambda: ref


def put_left(window_ref, base, side, ref):
    for j in range(3):
        high, low = split(ref[j])
        for part, value in enumerate((high, low, high)):
            window_ref[base + j, :, 16 * side : 16 * side + 16, lanes(part)] = value


def kept_square(out_ref, total_ref, mask_ref, strip):
    for g in range(3):
        for e in range(19):
            out_ref[g, e] = total_ref[g, e + 5, strip] * mask_ref[g, e].astype(F32)


def square_first_kernel(
    place_ref, mask_ref, given, out_ref, partial_ref, rest_ref,
    window_ref, narrow_ref, right_ref, total_ref,
):
    slabs, rows, last = given[:8], given[8:16], given[16]
    blank_corners(right_ref, 13)
    total_ref[...] = jnp.zeros_like(total_ref)
    for n, wait in enumerate(slabs):
        at = place_ref[5 + n] * 16
        put_right(right_ref, ((at, True), (128 + at, True), (256 + at, False)), wait())
    for n in range(4):
        for side in range(2):
            put_left(window_ref, 3 * n, side, rows[2 * n + side]())
        for j in range(3):
            r = place_ref[n] * 3 + j
            left = window_ref[3 * n + j].reshape(13 * 32, 384)
            add_row(left, right_ref[r], total_ref, r, slice(0, 32))
    put_left(narrow_ref, 0, 0, last())
    for j in range(3):
        r = place_ref[4] * 3 + j
        rest_ref[j] = right_ref[r]
        left = narrow_ref[j].reshape(13 * 16, 384)
        add_row(left, right_ref[r], total_ref, r, slice(16, 32))
    partial_ref[...] = total_ref[:, :, 0:16]
    kept_square(out_ref, total_ref, mask_ref, slice(16, 32))


def square_second_kernel(place_ref, mask_ref, given, out_ref, narrow_ref):
    last, rest, before = given
    put_left(narrow_ref, 0, 0, last())
    right_ref, total_ref = rest(), before()
    for j in range(3):
        left = narrow_ref[j].reshape(13 * 16, 384)
        add_row(left, right_ref[j], total_ref, place_ref[4] * 3 + j, slice(0, 16))
    kept_square(out_ref, total_ref, mask_ref, slice(0, 16))


def fill_half(right_ref, chips, slabs, core):
    blank_corners(right_ref, 19)
    zero = jnp.zeros((21, 16, 384), BF16)
    for n, chip in enumerate(chips):
        other = lax.rem(chip + 2, 4)
        for k in range(2):
            right_ref[:, pl.ds(pl.multiple_of(128 + 32 * other + 16 * k, 16), 16), :] = zero
        for k, slab in ((core, slabs[n]), (1 - core, slabs[2 + n])):
            place = 32 * chip + 16 * k
            again = 32 * other + 16 * k
            put_right(right_ref, ((place, True), (again, True), (128 + place, False)), slab())


def cube_first_kernel(place_ref, given, total_ref, next_ref, window_ref, right_ref):
    rows, slabs = given[:7], given[7:]
    low_y, core = place_ref[7], place_ref[8]
    fill_half(right_ref, (low_y, 3 - low_y), slabs, core)
    chip = lax.broadcasted_iota(jnp.int32, (208, 128), 1) // 32
    mine = (chip == low_y) | (chip == 3 - low_y)
    blocks = window_ref.shape[1:3] + (128,)
    for n, wait in enumerate(rows):
        base = place_ref[n] * 3
        ref = wait()
        for j in range(3):
            values = ref[j].reshape(208, 128)
            rounded = values.astype(BF16)
            high = rounded.astype(F32)
            low = pltpu.roll(values - high, 64, 1)
            first = jnp.where(mine, high, low).astype(BF16)
            second = jnp.where(mine, low, high).astype(BF16)
            window_ref[base + j, :, :, lanes(0)] = first.reshape(blocks)
            window_ref[base + j, :, :, lanes(1)] = rounded.reshape(blocks)
            next_ref[base + j, :, :, lanes(0)] = second.reshape(blocks)
            next_ref[base + j, :, :, lanes(1)] = rounded.reshape(blocks)
    total_ref[...] = jnp.zeros_like(total_ref)
    all_rows(window_ref, right_ref, total_ref)


def cube_second_kernel(place_ref, mask_ref, given, out_ref, right_ref, total_ref):
    before, window, own, slabs = given[0], given[1], given[2], given[3:]
    low_y, core = place_ref[7], place_ref[8]
    fill_half(right_ref, (low_y ^ 1, (3 - low_y) ^ 1), slabs, core)
    total_ref[...] = before()[...]
    window_ref, own_ref = window(), own()
    all_rows(window_ref, right_ref, total_ref)
    for g in range(3):
        for f in range(25):
            value = -2.0 * total_ref[g, f + 5]
            if 3 <= f < 22:
                value = 3.0 * own_ref[g, f - 3] + value
            out_ref[g, f] = value * mask_ref[g, f].astype(F32)


SMEM = pl.BlockSpec(memory_space=pltpu.SMEM)
VMEM = pl.BlockSpec(memory_space=pltpu.VMEM)
IN_HBM = pl.BlockSpec(memory_space=pltpu.HBM)
MIB = 1024 * 1024
LARGE, SMALL = 60, 24


def call(kernel, scalars, given, out_shape, scratch, limit, fetch):
    arrays, views, held = [], [], []
    for item in given:
        array, part = item if isinstance(item, tuple) else (item, None)
        known = [n for n, other in enumerate(arrays) if other is array]
        if not known:
            arrays.append(array)
        views.append((known[0] if known else len(arrays) - 1, part))
        held.append(pltpu.VMEM(array.shape if part is None else array.shape[1:], array.dtype))
    first = len(scalars)
    last = first + len(arrays)
    extra = held + [pltpu.SemaphoreType.DMA((len(held),))] if fetch else []

    def whole(*refs):
        parts = [refs[first + n] if p is None else refs[first + n].at[p] for n, p in views]
        end = len(refs) - len(extra)
        waits = fetched(parts, refs[end:-1], refs[-1]) if fetch else [here(p) for p in parts]
        kernel(*refs[:first], waits, *refs[last:end])

    return pl.pallas_call(
        whole,
        out_shape=out_shape,
        in_specs=[SMEM] * first + [IN_HBM if fetch else VMEM] * len(arrays),
        out_specs=jax.tree.map(lambda _: VMEM, out_shape),
        scratch_shapes=scratch + extra,
        compiler_params=pltpu.CompilerParams(vmem_limit_bytes=limit * MIB),
        cost_estimate=pl.CostEstimate(flops=1000000, bytes_accessed=1000, transcendentals=0),
    )(*scalars, *arrays)


def body(x_band, x_mask, sq_mask, cube_mask):
    high_y = lax.axis_index("row") % 2
    low_y, core = lax.axis_index("col") // 2, lax.axis_index("col") % 2

    own = pl.pallas_call(
        mask_kernel,
        out_shape=jax.ShapeDtypeStruct(x_band.shape, F32),
        in_specs=[SMEM, VMEM],
        out_specs=VMEM,
    )(x_mask, x_band)

    own_m, pair_m, below_o, above_o = together(
        send(own, MIRROR), send(own, FLIP), send(own, UP), send(own, DOWN)
    )
    both = jnp.stack([own, own_m])
    pair_o = send(own_m, FLIP)
    after, twin = send(both, NEXT), send(both, SIBLING)
    pair_o, below_m, above_m = together(pair_o, send(own_m, UP), send(own_m, DOWN))
    after, beside_m = together(after, send(pair_m, ACROSS))
    beside_o, beside_m = together(send(pair_o, ACROSS), beside_m)
    twin_after = send(after, SIBLING)

    chips = jnp.stack([low_y, 3 - low_y, low_y ^ 1, (3 - low_y) ^ 1])
    orbitals = jnp.concatenate([2 * chips + core, 2 * chips + 1 - core])
    pair_at, beside_at = 3 - 2 * high_y, 1 + 2 * high_y
    square_rows = jnp.stack([jnp.int32(0), jnp.int32(4), jnp.int32(2), pair_at, beside_at])
    square_places = jnp.concatenate([square_rows, orbitals]).astype(jnp.int32)
    cube_places = [1, 5, 3, pair_at + 1, beside_at + 1, 6 - 6 * high_y, 6 * high_y, low_y, core]
    cube_places = jnp.stack([jnp.int32(v) for v in cube_places])

    left = [(array, part) for array in (both, after, twin, twin_after) for part in (0, 1)]

    square_shape = jax.ShapeDtypeStruct((3, 19, 16, 128), F32)
    square_m, partial, rest = call(
        square_first_kernel,
        (square_places, sq_mask),
        left
        + [below_o, below_m, above_o, above_m, (both, 0), (both, 1), pair_o, pair_m, beside_m],
        (
            square_shape,
            jax.ShapeDtypeStruct((3, 29, 16, 128), F32),
            jax.ShapeDtypeStruct((3, 384, 384), BF16),
        ),
        [
            pltpu.VMEM((12, 13, 32, 384), BF16),
            pltpu.VMEM((3, 13, 16, 384), BF16),
            pltpu.VMEM((15, 384, 384), BF16),
            pltpu.VMEM((3, 29, 32, 128), F32),
        ],
        LARGE,
        True,
    )
    next_m = send(square_m, NEXT)
    twin_m, beside_o = together(send(square_m, SIBLING), beside_o)
    square_o = call(
        square_second_kernel,
        (square_places, sq_mask),
        [beside_o, rest, partial],
        square_shape,
        [pltpu.VMEM((3, 13, 16, 384), BF16)],
        LARGE,
        True,
    )
    twin_o, next_o = send(square_o, SIBLING), send(square_o, NEXT)
    far_a, far_b = send(pair_o, AGAINST), send(beside_o, ACROSS)
    total, window = call(
        cube_first_kernel,
        (cube_places,),
        [below_o, above_o, (both, 0), pair_o, beside_o, far_a, far_b]
        + [square_o, square_m, twin_o, twin_m],
        (
            jax.ShapeDtypeStruct((3, 35, 16, 128), F32),
            jax.ShapeDtypeStruct((21, 13, 16, 256), BF16),
        ),
        [pltpu.VMEM((21, 13, 16, 256), BF16), pltpu.VMEM((21, 256, 384), BF16)],
        SMALL,
        False,
    )
    total, next_o = together(total, next_o)
    return call(
        cube_second_kernel,
        (cube_places, cube_mask),
        [total, window, square_o, next_o, next_m, send(next_o, SIBLING), send(next_m, SIBLING)],
        jax.ShapeDtypeStruct((3, 25, 16, 128), F32),
        [pltpu.VMEM((21, 256, 384), BF16), pltpu.VMEM((3, 35, 16, 128), F32)],
        SMALL,
        False,
    )


def solution(mesh):
    return jax.shard_map(
        body,
        mesh=mesh,
        in_specs=(P("row", None, "col", None), P("row", None), P("row", None), P("row", None)),
        out_specs=P("row", None, "col", None),
        check_vma=False,
    )
```

```python
import functools

import jax
import jax.numpy as jnp
from jax import lax
from jax.experimental import pallas as pl
from jax.experimental.pallas import tpu as pltpu
from jax.sharding import PartitionSpec as P

Z, X, YH, YL, CORES = 12, 4, 2, 4, 2
CHAIN = Z * X
AXES = ("row", "col")
F32, BF16 = jnp.float32, jnp.bfloat16


def pairs(target):
    listed = []
    for c in range(CHAIN):
        for yh in range(YH):
            for yl in range(YL):
                for core in range(CORES):
                    to = target(c, yh, yl, core)
                    if to is not None:
                        tc, th, tl, tk = to
                        source = ((c * YH + yh) * YL + yl) * CORES + core
                        listed.append((source, (((tc % CHAIN) * YH + th) * YL + tl) * CORES + tk))
    return listed


UP = pairs(lambda c, h, l, k: (c + 1, h, l, k))
DOWN = pairs(lambda c, h, l, k: (c - 1, h, l, k))
ACROSS = pairs(lambda c, h, l, k: (c + 1 if h == 0 else c - 1, h, l, k))
AGAINST = pairs(lambda c, h, l, k: (c - 1 if h == 0 else c + 1, h, l, k))
FLIP = pairs(lambda c, h, l, k: (c, 1 - h, 3 - l, k))
MIRROR = pairs(lambda c, h, l, k: (c, h, 3 - l, k))
NEXT = pairs(lambda c, h, l, k: (c, h, l ^ 1, k))
SIBLING = pairs(lambda c, h, l, k: (c, h, l, 1 - k))


def send(array, which):
    return lax.ppermute(array, AXES, which)


def together(*arrays):
    return lax.optimization_barrier(arrays)


def split(values):
    high = values.astype(BF16)
    return high, (values - high.astype(F32)).astype(BF16)


def mask_kernel(mask_ref, x_ref, out_ref):
    for g in range(x_ref.shape[0]):
        for d in range(x_ref.shape[1]):
            out_ref[g, d] = x_ref[g, d] * mask_ref[g, d].astype(F32)


def lanes(g):
    return slice(128 * g, 128 * (g + 1))


def blank_corners(right_ref, blocks):
    for g in range(3):
        for r in range(blocks + 2):
            if not 0 <= r - g < blocks:
                right_ref[r, :, lanes(g)] = jnp.zeros((right_ref.shape[1], 128), BF16)


def put_right(right_ref, at, slab):
    blocks = slab.shape[1]
    for g in range(3):
        high, low = split(slab[g])
        for first, is_high in at:
            spot = pl.ds(pl.multiple_of(first, 16), 16)
            right_ref[g : g + blocks, spot, lanes(g)] = high if is_high else low


def accumulate(pieces, total_ref, rows, firsts):
    for (left, right), r in zip(pieces, firsts):
        product = jnp.dot(left, right, preferred_element_type=F32).reshape(13, rows, 384)
        for g in range(3):
            total_ref[g, pl.ds(r + 2 - g, 13)] += product[:, :, lanes(g)]


def all_rows(window_ref, right_ref, total_ref):
    count, _, rows, depth = window_ref.shape
    pieces = ((window_ref[r].reshape(13 * rows, depth), right_ref[r]) for r in range(count))
    accumulate(pieces, total_ref, rows, range(count))


def fetched(given, scratch, semaphores):
    copies = [
        pltpu.make_async_copy(ref, held, semaphores.at[n])
        for n, (ref, held) in enumerate(zip(given, scratch))
    ]
    for copy in copies:
        copy.start()

    def arrived(copy, held):
        def wait():
            copy.wait()
            return held

        return wait

    return [arrived(copy, held) for copy, held in zip(copies, scratch)]


def here(ref):
    return lambda: ref


def put_left(window_ref, base, side, ref):
    for j in range(3):
        high, low = split(ref[j])
        for part, value in enumerate((high, low, high)):
            window_ref[base + j, :, 16 * side : 16 * side + 16, lanes(part)] = value


def square_first_kernel(
    place_ref, given, total_ref, rest_ref, window_ref, right_ref
):
    rows, slabs = given[:8], given[8:]
    blank_corners(right_ref, 13)
    total_ref[...] = jnp.zeros_like(total_ref)
    for n, wait in enumerate(slabs):
        at = place_ref[5 + n] * 16
        put_right(right_ref, ((at, True), (128 + at, True), (256 + at, False)), wait())
    for n in range(4):
        for side in range(2):
            put_left(window_ref, 3 * n, side, rows[2 * n + side]())
    for j in range(3):
        rest_ref[j] = right_ref[place_ref[4] * 3 + j]
    firsts = [place_ref[n] * 3 + j for n in range(4) for j in range(3)]
    pieces = (
        (window_ref[n].reshape(13 * 32, 384), right_ref[r]) for n, r in enumerate(firsts)
    )
    accumulate(pieces, total_ref, 32, firsts)


def square_second_kernel(place_ref, mask_ref, given, out_ref, window_ref):
    before, rest, beside_o, beside_m = given
    put_left(window_ref, 0, 0, beside_o())
    put_left(window_ref, 0, 1, beside_m())
    total_ref, right_ref = before(), rest()
    firsts = [place_ref[4] * 3 + j for j in range(3)]
    pieces = ((window_ref[j].reshape(13 * 32, 384), right_ref[j]) for j in range(3))
    accumulate(pieces, total_ref, 32, firsts)
    for g in range(3):
        for e in range(19):
            kept = mask_ref[g, e].astype(F32)
            for side in range(2):
                out_ref[side, g, e] = total_ref[g, e + 5, 16 * side : 16 * side + 16] * kept


def fill_half(right_ref, chips, slabs, core):
    blank_corners(right_ref, 19)
    zero = jnp.zeros((21, 16, 384), BF16)
    for n, chip in enumerate(chips):
        other = lax.rem(chip + 2, 4)
        for k in range(2):
            right_ref[:, pl.ds(pl.multiple_of(128 + 32 * other + 16 * k, 16), 16), :] = zero
        for k, slab in ((core, slabs[n]), (1 - core, slabs[2 + n])):
            place = 32 * chip + 16 * k
            again = 32 * other + 16 * k
            put_right(right_ref, ((place, True), (again, True), (128 + place, False)), slab())


def cube_first_kernel(place_ref, given, total_ref, next_ref, window_ref, right_ref):
    rows, slabs = given[:7], given[7:]
    low_y, core = place_ref[7], place_ref[8]
    fill_half(right_ref, (low_y, 3 - low_y), slabs, core)
    chip = lax.broadcasted_iota(jnp.int32, (208, 128), 1) // 32
    mine = (chip == low_y) | (chip == 3 - low_y)
    blocks = window_ref.shape[1:3] + (128,)
    for n, wait in enumerate(rows):
        base = place_ref[n] * 3
        ref = wait()
        for j in range(3):
            values = ref[j].reshape(208, 128)
            rounded = values.astype(BF16)
            high = rounded.astype(F32)
            low = pltpu.roll(values - high, 64, 1)
            first = jnp.where(mine, high, low).astype(BF16)
            second = jnp.where(mine, low, high).astype(BF16)
            window_ref[base + j, :, :, lanes(0)] = first.reshape(blocks)
            window_ref[base + j, :, :, lanes(1)] = rounded.reshape(blocks)
            next_ref[base + j, :, :, lanes(0)] = second.reshape(blocks)
            next_ref[base + j, :, :, lanes(1)] = rounded.reshape(blocks)
    total_ref[...] = jnp.zeros_like(total_ref)
    all_rows(window_ref, right_ref, total_ref)


def cube_second_kernel(place_ref, mask_ref, given, out_ref, right_ref, total_ref):
    before, window, own, slabs = given[0], given[1], given[2], given[3:]
    low_y, core = place_ref[7], place_ref[8]
    fill_half(right_ref, (low_y ^ 1, (3 - low_y) ^ 1), slabs, core)
    total_ref[...] = before()[...]
    window_ref, own_ref = window(), own()
    all_rows(window_ref, right_ref, total_ref)
    for g in range(3):
        for f in range(25):
            value = -2.0 * total_ref[g, f + 5]
            if 3 <= f < 22:
                value = 3.0 * own_ref[g, f - 3] + value
            out_ref[g, f] = value * mask_ref[g, f].astype(F32)


SMEM = pl.BlockSpec(memory_space=pltpu.SMEM)
VMEM = pl.BlockSpec(memory_space=pltpu.VMEM)
IN_HBM = pl.BlockSpec(memory_space=pltpu.HBM)
MIB = 1024 * 1024
LARGE, SMALL = 60, 24


def call(kernel, scalars, given, out_shape, scratch, limit, fetch):
    arrays, views, held = [], [], []
    for item in given:
        array, part = item if isinstance(item, tuple) else (item, None)
        known = [n for n, other in enumerate(arrays) if other is array]
        if not known:
            arrays.append(array)
        views.append((known[0] if known else len(arrays) - 1, part))
        held.append(pltpu.VMEM(array.shape if part is None else array.shape[1:], array.dtype))
    first = len(scalars)
    last = first + len(arrays)
    extra = held + [pltpu.SemaphoreType.DMA((len(held),))] if fetch else []

    def whole(*refs):
        parts = [refs[first + n] if p is None else refs[first + n].at[p] for n, p in views]
        end = len(refs) - len(extra)
        waits = fetched(parts, refs[end:-1], refs[-1]) if fetch else [here(p) for p in parts]
        kernel(*refs[:first], waits, *refs[last:end])

    return pl.pallas_call(
        whole,
        out_shape=out_shape,
        in_specs=[SMEM] * first + [IN_HBM if fetch else VMEM] * len(arrays),
        out_specs=jax.tree.map(lambda _: VMEM, out_shape),
        scratch_shapes=scratch + extra,
        compiler_params=pltpu.CompilerParams(vmem_limit_bytes=limit * MIB),
        cost_estimate=pl.CostEstimate(flops=1000000, bytes_accessed=1000, transcendentals=0),
    )(*scalars, *arrays)


def body(x_band, x_mask, sq_mask, cube_mask):
    high_y = lax.axis_index("row") % 2
    low_y, core = lax.axis_index("col") // 2, lax.axis_index("col") % 2

    own = pl.pallas_call(
        mask_kernel,
        out_shape=jax.ShapeDtypeStruct(x_band.shape, F32),
        in_specs=[SMEM, VMEM],
        out_specs=VMEM,
    )(x_mask, x_band)

    own_m, pair_m, below_o, above_o = together(
        send(own, MIRROR), send(own, FLIP), send(own, UP), send(own, DOWN)
    )
    both = jnp.stack([own, own_m])
    pair_o = send(own_m, FLIP)
    after, twin = send(both, NEXT), send(both, SIBLING)
    pair_o, below_m, above_m = together(pair_o, send(own_m, UP), send(own_m, DOWN))
    after, beside_m = together(after, send(pair_m, ACROSS))
    beside_o, twin_after = send(pair_o, ACROSS), send(after, SIBLING)

    chips = jnp.stack([low_y, 3 - low_y, low_y ^ 1, (3 - low_y) ^ 1])
    orbitals = jnp.concatenate([2 * chips + core, 2 * chips + 1 - core])
    pair_at, beside_at = 3 - 2 * high_y, 1 + 2 * high_y
    square_rows = jnp.stack([jnp.int32(0), jnp.int32(4), jnp.int32(2), pair_at, beside_at])
    square_places = jnp.concatenate([square_rows, orbitals]).astype(jnp.int32)
    cube_places = [1, 5, 3, pair_at + 1, beside_at + 1, 6 - 6 * high_y, 6 * high_y, low_y, core]
    cube_places = jnp.stack([jnp.int32(v) for v in cube_places])

    left = [(array, part) for array in (both, after, twin, twin_after) for part in (0, 1)]

    partial, rest = call(
        square_first_kernel,
        (square_places,),
        [below_o, below_m, above_o, above_m, (both, 0), (both, 1), pair_o, pair_m] + left,
        (
            jax.ShapeDtypeStruct((3, 29, 32, 128), F32),
            jax.ShapeDtypeStruct((3, 384, 384), BF16),
        ),
        [pltpu.VMEM((12, 13, 32, 384), BF16), pltpu.VMEM((15, 384, 384), BF16)],
        LARGE,
        True,
    )
    square = call(
        square_second_kernel,
        (square_places, sq_mask),
        [partial, rest, beside_o, beside_m],
        jax.ShapeDtypeStruct((2, 3, 19, 16, 128), F32),
        [pltpu.VMEM((3, 13, 32, 384), BF16)],
        LARGE,
        True,
    )
    square_after = send(square, NEXT)
    square_twin, pair_late, beside_late = together(send(square, SIBLING), pair_o, beside_o)
    far_a, far_b = send(pair_late, AGAINST), send(beside_late, ACROSS)
    total, window = call(
        cube_first_kernel,
        (cube_places,),
        [below_o, above_o, (both, 0), pair_o, beside_o, far_a, far_b]
        + [(square, 0), (square, 1), (square_twin, 0), (square_twin, 1)],
        (
            jax.ShapeDtypeStruct((3, 35, 16, 128), F32),
            jax.ShapeDtypeStruct((21, 13, 16, 256), BF16),
        ),
        [pltpu.VMEM((21, 13, 16, 256), BF16), pltpu.VMEM((21, 256, 384), BF16)],
        SMALL,
        False,
    )
    total, square_after = together(total, square_after)
    after_twin = send(square_after, SIBLING)
    return call(
        cube_second_kernel,
        (cube_places, cube_mask),
        [total, window, (square, 0), (square_after, 0), (square_after, 1)]
        + [(after_twin, 0), (after_twin, 1)],
        jax.ShapeDtypeStruct((3, 25, 16, 128), F32),
        [pltpu.VMEM((21, 256, 384), BF16), pltpu.VMEM((3, 35, 16, 128), F32)],
        SMALL,
        False,
    )


def solution(mesh):
    return jax.shard_map(
        body,
        mesh=mesh,
        in_specs=(P("row", None, "col", None), P("row", None), P("row", None), P("row", None)),
        out_specs=P("row", None, "col", None),
        check_vma=False,
    )
```

```python
import functools

import jax
import jax.numpy as jnp
from jax import lax
from jax.experimental import pallas as pl
from jax.experimental.pallas import tpu as pltpu
from jax.sharding import PartitionSpec as P

Z, X, YH, YL, CORES = 12, 4, 2, 4, 2
CHAIN = Z * X
AXES = ("row", "col")
F32, BF16 = jnp.float32, jnp.bfloat16


def pairs(target):
    listed = []
    for c in range(CHAIN):
        for yh in range(YH):
            for yl in range(YL):
                for core in range(CORES):
                    to = target(c, yh, yl, core)
                    if to is not None:
                        tc, th, tl, tk = to
                        source = ((c * YH + yh) * YL + yl) * CORES + core
                        listed.append((source, (((tc % CHAIN) * YH + th) * YL + tl) * CORES + tk))
    return listed


UP = pairs(lambda c, h, l, k: (c + 1, h, l, k))
DOWN = pairs(lambda c, h, l, k: (c - 1, h, l, k))
ACROSS = pairs(lambda c, h, l, k: (c + 1 if h == 0 else c - 1, h, l, k))
AGAINST = pairs(lambda c, h, l, k: (c - 1 if h == 0 else c + 1, h, l, k))
FLIP = pairs(lambda c, h, l, k: (c, 1 - h, 3 - l, k))
MIRROR = pairs(lambda c, h, l, k: (c, h, 3 - l, k))
NEXT = pairs(lambda c, h, l, k: (c, h, l ^ 1, k))
SIBLING = pairs(lambda c, h, l, k: (c, h, l, 1 - k))


def send(array, which):
    return lax.ppermute(array, AXES, which)


def together(*arrays):
    return lax.optimization_barrier(arrays)


def split(values):
    high = values.astype(BF16)
    return high, (values - high.astype(F32)).astype(BF16)


def mask_kernel(mask_ref, x_ref, out_ref):
    for g in range(x_ref.shape[0]):
        for d in range(x_ref.shape[1]):
            out_ref[g, d] = x_ref[g, d] * mask_ref[g, d].astype(F32)


def lanes(g):
    return slice(128 * g, 128 * (g + 1))


def blank_corners(right_ref, blocks):
    for g in range(3):
        for r in range(blocks + 2):
            if not 0 <= r - g < blocks:
                right_ref[r, :, lanes(g)] = jnp.zeros((right_ref.shape[1], 128), BF16)


def put_right(right_ref, at, slab):
    blocks = slab.shape[1]
    for g in range(3):
        high, low = split(slab[g])
        for first, is_high in at:
            spot = pl.ds(pl.multiple_of(first, 16), 16)
            right_ref[g : g + blocks, spot, lanes(g)] = high if is_high else low


def accumulate(pieces, total_ref, rows, firsts):
    for (left, right), r in zip(pieces, firsts):
        product = jnp.dot(left, right, preferred_element_type=F32).reshape(13, rows, 384)
        for g in range(3):
            total_ref[g, pl.ds(r + 2 - g, 13)] += product[:, :, lanes(g)]


def all_rows(window_ref, right_ref, total_ref):
    count, _, rows, depth = window_ref.shape
    pieces = ((window_ref[r].reshape(13 * rows, depth), right_ref[r]) for r in range(count))
    accumulate(pieces, total_ref, rows, range(count))


def fetched(given, scratch, semaphores):
    copies = [
        pltpu.make_async_copy(ref, held, semaphores.at[n])
        for n, (ref, held) in enumerate(zip(given, scratch))
    ]
    for copy in copies:
        copy.start()

    def arrived(copy, held):
        def wait():
            copy.wait()
            return held

        return wait

    return [arrived(copy, held) for copy, held in zip(copies, scratch)]


def here(ref):
    return lambda: ref


def put_left(window_ref, base, side, ref):
    for j in range(3):
        high, low = split(ref[j])
        for part, value in enumerate((high, low, high)):
            window_ref[base + j, :, 16 * side : 16 * side + 16, lanes(part)] = value


def square_first_kernel(
    place_ref, given, total_ref, rest_ref, window_ref, right_ref
):
    rows, slabs = given[:8], given[8:]
    blank_corners(right_ref, 13)
    total_ref[...] = jnp.zeros_like(total_ref)
    for n, wait in enumerate(slabs):
        at = place_ref[5 + n] * 16
        put_right(right_ref, ((at, True), (128 + at, True), (256 + at, False)), wait())
    for n in range(4):
        for side in range(2):
            put_left(window_ref, 3 * n, side, rows[2 * n + side]())
    for j in range(3):
        rest_ref[j] = right_ref[place_ref[4] * 3 + j]
    firsts = [place_ref[n] * 3 + j for n in range(4) for j in range(3)]
    pieces = (
        (window_ref[n].reshape(13 * 32, 384), right_ref[r]) for n, r in enumerate(firsts)
    )
    accumulate(pieces, total_ref, 32, firsts)


def square_second_kernel(place_ref, mask_ref, given, out_ref, window_ref):
    before, rest, beside_o, beside_m = given
    put_left(window_ref, 0, 0, beside_o())
    put_left(window_ref, 0, 1, beside_m())
    total_ref, right_ref = before(), rest()
    firsts = [place_ref[4] * 3 + j for j in range(3)]
    pieces = ((window_ref[j].reshape(13 * 32, 384), right_ref[j]) for j in range(3))
    accumulate(pieces, total_ref, 32, firsts)
    for g in range(3):
        for e in range(19):
            kept = mask_ref[g, e].astype(F32)
            for side in range(2):
                out_ref[side, g, e] = total_ref[g, e + 5, 16 * side : 16 * side + 16] * kept


def fill_half(right_ref, chips, slabs, core):
    blank_corners(right_ref, 19)
    zero = jnp.zeros((21, 16, 384), BF16)
    for n, chip in enumerate(chips):
        other = lax.rem(chip + 2, 4)
        for k in range(2):
            right_ref[:, pl.ds(pl.multiple_of(128 + 32 * other + 16 * k, 16), 16), :] = zero
        for k, slab in ((core, slabs[n]), (1 - core, slabs[2 + n])):
            place = 32 * chip + 16 * k
            again = 32 * other + 16 * k
            put_right(right_ref, ((place, True), (again, True), (128 + place, False)), slab())


def cube_first_kernel(place_ref, given, total_ref, next_ref, window_ref, right_ref):
    rows, slabs = given[:7], given[7:]
    low_y, core = place_ref[7], place_ref[8]
    fill_half(right_ref, (low_y, 3 - low_y), slabs, core)
    chip = lax.broadcasted_iota(jnp.int32, (208, 128), 1) // 32
    mine = (chip == low_y) | (chip == 3 - low_y)
    blocks = window_ref.shape[1:3] + (128,)
    for n, wait in enumerate(rows):
        base = place_ref[n] * 3
        ref = wait()
        for j in range(3):
            values = ref[j].reshape(208, 128)
            rounded = values.astype(BF16)
            high = rounded.astype(F32)
            low = pltpu.roll(values - high, 64, 1)
            first = jnp.where(mine, high, low).astype(BF16)
            second = jnp.where(mine, low, high).astype(BF16)
            window_ref[base + j, :, :, lanes(0)] = first.reshape(blocks)
            window_ref[base + j, :, :, lanes(1)] = rounded.reshape(blocks)
            next_ref[base + j, :, :, lanes(0)] = second.reshape(blocks)
            next_ref[base + j, :, :, lanes(1)] = rounded.reshape(blocks)
    total_ref[...] = jnp.zeros_like(total_ref)
    all_rows(window_ref, right_ref, total_ref)


def cube_second_kernel(place_ref, mask_ref, given, out_ref, right_ref, total_ref):
    before, window, own, slabs = given[0], given[1], given[2], given[3:]
    low_y, core = place_ref[7], place_ref[8]
    fill_half(right_ref, (low_y ^ 1, (3 - low_y) ^ 1), slabs, core)
    total_ref[...] = before()[...]
    window_ref, own_ref = window(), own()
    all_rows(window_ref, right_ref, total_ref)
    for g in range(3):
        for f in range(25):
            value = -2.0 * total_ref[g, f + 5]
            if 3 <= f < 22:
                value = 3.0 * own_ref[g, f - 3] + value
            out_ref[g, f] = value * mask_ref[g, f].astype(F32)


SMEM = pl.BlockSpec(memory_space=pltpu.SMEM)
VMEM = pl.BlockSpec(memory_space=pltpu.VMEM)
IN_HBM = pl.BlockSpec(memory_space=pltpu.HBM)
MIB = 1024 * 1024
LARGE, SMALL = 60, 24


def call(kernel, scalars, given, out_shape, scratch, limit, fetch):
    arrays, views, held = [], [], []
    for item in given:
        array, part = item if isinstance(item, tuple) else (item, None)
        known = [n for n, other in enumerate(arrays) if other is array]
        if not known:
            arrays.append(array)
        views.append((known[0] if known else len(arrays) - 1, part))
        held.append(pltpu.VMEM(array.shape if part is None else array.shape[1:], array.dtype))
    first = len(scalars)
    last = first + len(arrays)
    extra = held + [pltpu.SemaphoreType.DMA((len(held),))] if fetch else []

    def whole(*refs):
        parts = [refs[first + n] if p is None else refs[first + n].at[p] for n, p in views]
        end = len(refs) - len(extra)
        waits = fetched(parts, refs[end:-1], refs[-1]) if fetch else [here(p) for p in parts]
        kernel(*refs[:first], waits, *refs[last:end])

    return pl.pallas_call(
        whole,
        out_shape=out_shape,
        in_specs=[SMEM] * first + [IN_HBM if fetch else VMEM] * len(arrays),
        out_specs=jax.tree.map(lambda _: VMEM, out_shape),
        scratch_shapes=scratch + extra,
        compiler_params=pltpu.CompilerParams(vmem_limit_bytes=limit * MIB),
        cost_estimate=pl.CostEstimate(flops=1000000, bytes_accessed=1000, transcendentals=0),
    )(*scalars, *arrays)


def body(x_band, x_mask, sq_mask, cube_mask):
    high_y = lax.axis_index("row") % 2
    low_y, core = lax.axis_index("col") // 2, lax.axis_index("col") % 2

    own = pl.pallas_call(
        mask_kernel,
        out_shape=jax.ShapeDtypeStruct(x_band.shape, F32),
        in_specs=[SMEM, VMEM],
        out_specs=VMEM,
    )(x_mask, x_band)

    own_m, pair_m = together(send(own, MIRROR), send(own, FLIP))
    both = jnp.stack([own, own_m])
    pair_o = send(own_m, FLIP)
    after, twin = send(both, NEXT), send(both, SIBLING)
    after, pair_o, beside_m = together(after, pair_o, send(pair_m, ACROSS))
    below, above = send(both, UP), send(both, DOWN)
    beside_o, twin_after = send(pair_o, ACROSS), send(after, SIBLING)

    chips = jnp.stack([low_y, 3 - low_y, low_y ^ 1, (3 - low_y) ^ 1])
    orbitals = jnp.concatenate([2 * chips + core, 2 * chips + 1 - core])
    pair_at, beside_at = 3 - 2 * high_y, 1 + 2 * high_y
    square_rows = jnp.stack([jnp.int32(0), jnp.int32(4), jnp.int32(2), pair_at, beside_at])
    square_places = jnp.concatenate([square_rows, orbitals]).astype(jnp.int32)
    cube_places = [1, 5, 3, pair_at + 1, beside_at + 1, 6 - 6 * high_y, 6 * high_y, low_y, core]
    cube_places = jnp.stack([jnp.int32(v) for v in cube_places])

    left = [(array, part) for array in (both, after, twin, twin_after) for part in (0, 1)]

    partial, rest = call(
        square_first_kernel,
        (square_places,),
        [(below, 0), (below, 1), (above, 0), (above, 1), (both, 0), (both, 1), pair_o, pair_m]
        + left,
        (
            jax.ShapeDtypeStruct((3, 29, 32, 128), F32),
            jax.ShapeDtypeStruct((3, 384, 384), BF16),
        ),
        [pltpu.VMEM((12, 13, 32, 384), BF16), pltpu.VMEM((15, 384, 384), BF16)],
        LARGE,
        True,
    )
    square = call(
        square_second_kernel,
        (square_places, sq_mask),
        [partial, rest, beside_o, beside_m],
        jax.ShapeDtypeStruct((2, 3, 19, 16, 128), F32),
        [pltpu.VMEM((3, 13, 32, 384), BF16)],
        LARGE,
        True,
    )
    square_after = send(square, NEXT)
    square_twin, pair_late, beside_late = together(send(square, SIBLING), pair_o, beside_o)
    far_a, far_b = send(pair_late, AGAINST), send(beside_late, ACROSS)
    total, window = call(
        cube_first_kernel,
        (cube_places,),
        [(below, 0), (above, 0), (both, 0), pair_o, beside_o, far_a, far_b]
        + [(square, 0), (square, 1), (square_twin, 0), (square_twin, 1)],
        (
            jax.ShapeDtypeStruct((3, 35, 16, 128), F32),
            jax.ShapeDtypeStruct((21, 13, 16, 256), BF16),
        ),
        [pltpu.VMEM((21, 13, 16, 256), BF16), pltpu.VMEM((21, 256, 384), BF16)],
        SMALL,
        False,
    )
    total, square_after = together(total, square_after)
    after_twin = send(square_after, SIBLING)
    return call(
        cube_second_kernel,
        (cube_places, cube_mask),
        [total, window, (square, 0), (square_after, 0), (square_after, 1)]
        + [(after_twin, 0), (after_twin, 1)],
        jax.ShapeDtypeStruct((3, 25, 16, 128), F32),
        [pltpu.VMEM((21, 256, 384), BF16), pltpu.VMEM((3, 35, 16, 128), F32)],
        SMALL,
        False,
    )


def solution(mesh):
    return jax.shard_map(
        body,
        mesh=mesh,
        in_specs=(P("row", None, "col", None), P("row", None), P("row", None), P("row", None)),
        out_specs=P("row", None, "col", None),
        check_vma=False,
    )
```

```python
import functools

import jax
import jax.numpy as jnp
from jax import lax
from jax.experimental import pallas as pl
from jax.experimental.pallas import tpu as pltpu
from jax.sharding import PartitionSpec as P

Z, X, YH, YL, CORES = 12, 4, 2, 4, 2
CHAIN = Z * X
AXES = ("row", "col")
F32, BF16 = jnp.float32, jnp.bfloat16


def pairs(target):
    listed = []
    for c in range(CHAIN):
        for yh in range(YH):
            for yl in range(YL):
                for core in range(CORES):
                    to = target(c, yh, yl, core)
                    if to is not None:
                        tc, th, tl, tk = to
                        source = ((c * YH + yh) * YL + yl) * CORES + core
                        listed.append((source, (((tc % CHAIN) * YH + th) * YL + tl) * CORES + tk))
    return listed


UP = pairs(lambda c, h, l, k: (c + 1, h, l, k))
DOWN = pairs(lambda c, h, l, k: (c - 1, h, l, k))
ACROSS = pairs(lambda c, h, l, k: (c + 1 if h == 0 else c - 1, h, l, k))
AGAINST = pairs(lambda c, h, l, k: (c - 1 if h == 0 else c + 1, h, l, k))
FLIP = pairs(lambda c, h, l, k: (c, 1 - h, 3 - l, k))
MIRROR = pairs(lambda c, h, l, k: (c, h, 3 - l, k))
NEXT = pairs(lambda c, h, l, k: (c, h, l ^ 1, k))
SIBLING = pairs(lambda c, h, l, k: (c, h, l, 1 - k))


def send(array, which):
    return lax.ppermute(array, AXES, which)


def together(*arrays):
    return lax.optimization_barrier(arrays)


def split(values):
    high = values.astype(BF16)
    return high, (values - high.astype(F32)).astype(BF16)


def mask_kernel(mask_ref, x_ref, out_ref):
    for g in range(x_ref.shape[0]):
        for d in range(x_ref.shape[1]):
            out_ref[g, d] = x_ref[g, d] * mask_ref[g, d].astype(F32)


def lanes(g):
    return slice(128 * g, 128 * (g + 1))


def blank_corners(right_ref, blocks):
    for g in range(3):
        for r in range(blocks + 2):
            if not 0 <= r - g < blocks:
                right_ref[r, :, lanes(g)] = jnp.zeros((right_ref.shape[1], 128), BF16)


def put_right(right_ref, at, slab):
    blocks = slab.shape[1]
    for g in range(3):
        high, low = split(slab[g])
        for first, is_high in at:
            spot = pl.ds(pl.multiple_of(first, 16), 16)
            right_ref[g : g + blocks, spot, lanes(g)] = high if is_high else low


def accumulate(pieces, total_ref, rows, firsts):
    for (left, right), r in zip(pieces, firsts):
        product = jnp.dot(left, right, preferred_element_type=F32).reshape(13, rows, 384)
        for g in range(3):
            total_ref[g, pl.ds(r + 2 - g, 13)] += product[:, :, lanes(g)]


def all_rows(window_ref, right_ref, total_ref):
    count, _, rows, depth = window_ref.shape
    pieces = ((window_ref[r].reshape(13 * rows, depth), right_ref[r]) for r in range(count))
    accumulate(pieces, total_ref, rows, range(count))


def fetched(given, scratch, semaphores):
    copies = [
        pltpu.make_async_copy(ref, held, semaphores.at[n])
        for n, (ref, held) in enumerate(zip(given, scratch))
    ]
    for copy in copies:
        copy.start()

    def arrived(copy, held):
        def wait():
            copy.wait()
            return held

        return wait

    return [arrived(copy, held) for copy, held in zip(copies, scratch)]


def here(ref):
    return lambda: ref


def put_left(window_ref, base, side, ref):
    for j in range(3):
        high, low = split(ref[j])
        for part, value in enumerate((high, low, high)):
            window_ref[base + j, :, 16 * side : 16 * side + 16, lanes(part)] = value


def square_first_kernel(
    place_ref, given, total_ref, rest_ref, window_ref, right_ref
):
    slabs, rows = given[:8], given[8:]
    blank_corners(right_ref, 13)
    total_ref[...] = jnp.zeros_like(total_ref)
    for n, wait in enumerate(slabs):
        at = place_ref[5 + n] * 16
        put_right(right_ref, ((at, True), (128 + at, True), (256 + at, False)), wait())
    for n in range(4):
        for side in range(2):
            put_left(window_ref, 3 * n, side, rows[2 * n + side]())
        firsts = [place_ref[n] * 3 + j for j in range(3)]
        pieces = (
            (window_ref[3 * n + j].reshape(13 * 32, 384), right_ref[r])
            for j, r in enumerate(firsts)
        )
        accumulate(pieces, total_ref, 32, firsts)
    for j in range(3):
        rest_ref[j] = right_ref[place_ref[4] * 3 + j]


def square_second_kernel(place_ref, mask_ref, given, out_ref, window_ref):
    before, rest, beside_o, beside_m = given
    put_left(window_ref, 0, 0, beside_o())
    put_left(window_ref, 0, 1, beside_m())
    total_ref, right_ref = before(), rest()
    firsts = [place_ref[4] * 3 + j for j in range(3)]
    pieces = ((window_ref[j].reshape(13 * 32, 384), right_ref[j]) for j in range(3))
    accumulate(pieces, total_ref, 32, firsts)
    for g in range(3):
        for e in range(19):
            kept = mask_ref[g, e].astype(F32)
            for side in range(2):
                out_ref[side, g, e] = total_ref[g, e + 5, 16 * side : 16 * side + 16] * kept


def quartet(low_y):
    return low_y, 3 - low_y, low_y ^ 1, (3 - low_y) ^ 1


def fill_half(right_ref, chips, slabs, core):
    blank_corners(right_ref, 19)
    zero = jnp.zeros((21, 16, 384), BF16)
    for chip, slab in zip(chips, slabs):
        place = 32 * chip + 16 * core
        idle = 128 + 32 * chip + 16 * (1 - core)
        right_ref[:, pl.ds(pl.multiple_of(idle, 16), 16), :] = zero
        again = lax.rem(place + 16, 128)
        put_right(right_ref, ((place, True), (again, True), (128 + place, False)), slab())


def cube_first_kernel(place_ref, given, total_ref, next_ref, window_ref, right_ref):
    rows, slabs = given[:7], given[7:]
    low_y, core = place_ref[7], place_ref[8]
    fill_half(right_ref, quartet(low_y), slabs, core)
    mine = lax.broadcasted_iota(jnp.int32, (208, 128), 1) // 16 % 2 == core
    blocks = window_ref.shape[1:3] + (128,)
    for n, wait in enumerate(rows):
        base = place_ref[n] * 3
        ref = wait()
        for j in range(3):
            values = ref[j].reshape(208, 128)
            rounded = values.astype(BF16)
            high = rounded.astype(F32)
            low = pltpu.roll(values - high, 16, 1)
            first = jnp.where(mine, high, low).astype(BF16)
            second = jnp.where(mine, low, high).astype(BF16)
            window_ref[base + j, :, :, lanes(0)] = first.reshape(blocks)
            window_ref[base + j, :, :, lanes(1)] = rounded.reshape(blocks)
            next_ref[base + j, :, :, lanes(0)] = second.reshape(blocks)
            next_ref[base + j, :, :, lanes(1)] = rounded.reshape(blocks)
    total_ref[...] = jnp.zeros_like(total_ref)
    all_rows(window_ref, right_ref, total_ref)


def cube_second_kernel(place_ref, mask_ref, given, out_ref, right_ref, total_ref):
    before, window, own, slabs = given[0], given[1], given[2], given[3:]
    low_y, core = place_ref[7], place_ref[8]
    fill_half(right_ref, quartet(low_y), slabs, 1 - core)
    total_ref[...] = before()[...]
    window_ref, own_ref = window(), own()
    all_rows(window_ref, right_ref, total_ref)
    for g in range(3):
        for f in range(25):
            value = -2.0 * total_ref[g, f + 5]
            if 3 <= f < 22:
                value = 3.0 * own_ref[g, f - 3] + value
            out_ref[g, f] = value * mask_ref[g, f].astype(F32)


SMEM = pl.BlockSpec(memory_space=pltpu.SMEM)
VMEM = pl.BlockSpec(memory_space=pltpu.VMEM)
IN_HBM = pl.BlockSpec(memory_space=pltpu.HBM)
MIB = 1024 * 1024
LARGE, SMALL = 60, 24


def call(kernel, scalars, given, out_shape, scratch, limit, fetch):
    arrays, views, held = [], [], []
    for item in given:
        array, part = item if isinstance(item, tuple) else (item, None)
        known = [n for n, other in enumerate(arrays) if other is array]
        if not known:
            arrays.append(array)
        views.append((known[0] if known else len(arrays) - 1, part))
        held.append(pltpu.VMEM(array.shape if part is None else array.shape[1:], array.dtype))
    first = len(scalars)
    last = first + len(arrays)
    extra = held + [pltpu.SemaphoreType.DMA((len(held),))] if fetch else []

    def whole(*refs):
        parts = [refs[first + n] if p is None else refs[first + n].at[p] for n, p in views]
        end = len(refs) - len(extra)
        waits = fetched(parts, refs[end:-1], refs[-1]) if fetch else [here(p) for p in parts]
        kernel(*refs[:first], waits, *refs[last:end])

    return pl.pallas_call(
        whole,
        out_shape=out_shape,
        in_specs=[SMEM] * first + [IN_HBM if fetch else VMEM] * len(arrays),
        out_specs=jax.tree.map(lambda _: VMEM, out_shape),
        scratch_shapes=scratch + extra,
        compiler_params=pltpu.CompilerParams(vmem_limit_bytes=limit * MIB),
        cost_estimate=pl.CostEstimate(flops=1000000, bytes_accessed=1000, transcendentals=0),
    )(*scalars, *arrays)


def body(x_band, x_mask, sq_mask, cube_mask):
    high_y = lax.axis_index("row") % 2
    low_y, core = lax.axis_index("col") // 2, lax.axis_index("col") % 2

    own = pl.pallas_call(
        mask_kernel,
        out_shape=jax.ShapeDtypeStruct(x_band.shape, F32),
        in_specs=[SMEM, VMEM],
        out_specs=VMEM,
    )(x_mask, x_band)

    own_m, pair_m, below_o, above_o = together(
        send(own, MIRROR), send(own, FLIP), send(own, UP), send(own, DOWN)
    )
    both = jnp.stack([own, own_m])
    pair_o = send(own_m, FLIP)
    after, twin = send(both, NEXT), send(both, SIBLING)
    pair_o, below_m, above_m = together(pair_o, send(own_m, UP), send(own_m, DOWN))
    after, beside_m = together(after, send(pair_m, ACROSS))
    beside_o, twin_after = send(pair_o, ACROSS), send(after, SIBLING)

    chips = jnp.stack([low_y, 3 - low_y, low_y ^ 1, (3 - low_y) ^ 1])
    orbitals = jnp.concatenate([2 * chips + core, 2 * chips + 1 - core])
    pair_at, beside_at = 3 - 2 * high_y, 1 + 2 * high_y
    square_rows = jnp.stack([jnp.int32(0), jnp.int32(4), jnp.int32(2), pair_at, beside_at])
    square_places = jnp.concatenate([square_rows, orbitals]).astype(jnp.int32)
    cube_places = [1, 5, 3, pair_at + 1, beside_at + 1, 6 - 6 * high_y, 6 * high_y, low_y, core]
    cube_places = jnp.stack([jnp.int32(v) for v in cube_places])

    left = [(array, part) for array in (both, after, twin, twin_after) for part in (0, 1)]

    partial, rest = call(
        square_first_kernel,
        (square_places,),
        left + [below_o, below_m, above_o, above_m, (both, 0), (both, 1), pair_o, pair_m],
        (
            jax.ShapeDtypeStruct((3, 29, 32, 128), F32),
            jax.ShapeDtypeStruct((3, 384, 384), BF16),
        ),
        [pltpu.VMEM((12, 13, 32, 384), BF16), pltpu.VMEM((15, 384, 384), BF16)],
        LARGE,
        True,
    )
    square = call(
        square_second_kernel,
        (square_places, sq_mask),
        [partial, rest, beside_o, beside_m],
        jax.ShapeDtypeStruct((2, 3, 19, 16, 128), F32),
        [pltpu.VMEM((3, 13, 32, 384), BF16)],
        LARGE,
        True,
    )
    square_twin = send(square, SIBLING)
    square_after, far_a, far_b = together(
        send(square, NEXT), send(pair_o, AGAINST), send(beside_o, ACROSS)
    )
    total, window = call(
        cube_first_kernel,
        (cube_places,),
        [below_o, above_o, (both, 0), pair_o, beside_o, far_a, far_b]
        + [(square, 0), (square, 1), (square_after, 0), (square_after, 1)],
        (
            jax.ShapeDtypeStruct((3, 35, 16, 128), F32),
            jax.ShapeDtypeStruct((21, 13, 16, 256), BF16),
        ),
        [pltpu.VMEM((21, 13, 16, 256), BF16), pltpu.VMEM((21, 256, 384), BF16)],
        SMALL,
        False,
    )
    after_twin = send(square_after, SIBLING)
    return call(
        cube_second_kernel,
        (cube_places, cube_mask),
        [total, window, (square, 0), (square_twin, 0), (square_twin, 1)]
        + [(after_twin, 0), (after_twin, 1)],
        jax.ShapeDtypeStruct((3, 25, 16, 128), F32),
        [pltpu.VMEM((21, 256, 384), BF16), pltpu.VMEM((3, 35, 16, 128), F32)],
        SMALL,
        False,
    )


def solution(mesh):
    return jax.shard_map(
        body,
        mesh=mesh,
        in_specs=(P("row", None, "col", None), P("row", None), P("row", None), P("row", None)),
        out_specs=P("row", None, "col", None),
        check_vma=False,
    )
```

```python
import functools

import jax
import jax.numpy as jnp
from jax import lax
from jax.experimental import pallas as pl
from jax.experimental.pallas import tpu as pltpu
from jax.sharding import PartitionSpec as P

Z, X, YH, YL, CORES = 12, 4, 2, 4, 2
CHAIN = Z * X
AXES = ("row", "col")
F32, BF16 = jnp.float32, jnp.bfloat16


def pairs(target):
    listed = []
    for c in range(CHAIN):
        for yh in range(YH):
            for yl in range(YL):
                for core in range(CORES):
                    to = target(c, yh, yl, core)
                    if to is not None:
                        tc, th, tl, tk = to
                        source = ((c * YH + yh) * YL + yl) * CORES + core
                        listed.append((source, (((tc % CHAIN) * YH + th) * YL + tl) * CORES + tk))
    return listed


UP = pairs(lambda c, h, l, k: (c + 1, h, l, k))
DOWN = pairs(lambda c, h, l, k: (c - 1, h, l, k))
ACROSS = pairs(lambda c, h, l, k: (c + 1 if h == 0 else c - 1, h, l, k))
AGAINST = pairs(lambda c, h, l, k: (c - 1 if h == 0 else c + 1, h, l, k))
FLIP = pairs(lambda c, h, l, k: (c, 1 - h, 3 - l, k))
MIRROR = pairs(lambda c, h, l, k: (c, h, 3 - l, k))
NEXT = pairs(lambda c, h, l, k: (c, h, l ^ 1, k))
SIBLING = pairs(lambda c, h, l, k: (c, h, l, 1 - k))


def send(array, which):
    return lax.ppermute(array, AXES, which)


def together(*arrays):
    return lax.optimization_barrier(arrays)


def split(values):
    high = values.astype(BF16)
    return high, (values - high.astype(F32)).astype(BF16)


def mask_kernel(mask_ref, x_ref, out_ref):
    for g in range(x_ref.shape[0]):
        for d in range(x_ref.shape[1]):
            out_ref[g, d] = x_ref[g, d] * mask_ref[g, d].astype(F32)


def lanes(g):
    return slice(128 * g, 128 * (g + 1))


def blank_corners(right_ref, blocks):
    for g in range(3):
        for r in range(blocks + 2):
            if not 0 <= r - g < blocks:
                right_ref[r, :, lanes(g)] = jnp.zeros((right_ref.shape[1], 128), BF16)


def put_right(right_ref, at, slab):
    blocks = slab.shape[1]
    for g in range(3):
        high, low = split(slab[g])
        for first, is_high in at:
            spot = pl.ds(pl.multiple_of(first, 16), 16)
            right_ref[g : g + blocks, spot, lanes(g)] = high if is_high else low


def accumulate(pieces, total_ref, rows, firsts):
    for (left, right), r in zip(pieces, firsts):
        product = jnp.dot(left, right, preferred_element_type=F32).reshape(13, rows, 384)
        for g in range(3):
            total_ref[g, pl.ds(r + 2 - g, 13)] += product[:, :, lanes(g)]


def all_rows(window_ref, right_ref, total_ref):
    count, _, rows, depth = window_ref.shape
    pieces = ((window_ref[r].reshape(13 * rows, depth), right_ref[r]) for r in range(count))
    accumulate(pieces, total_ref, rows, range(count))


def fetched(given, scratch, semaphores):
    copies = [
        pltpu.make_async_copy(ref, held, semaphores.at[n])
        for n, (ref, held) in enumerate(zip(given, scratch))
    ]
    for copy in copies:
        copy.start()

    def arrived(copy, held):
        def wait():
            copy.wait()
            return held

        return wait

    return [arrived(copy, held) for copy, held in zip(copies, scratch)]


def here(ref):
    return lambda: ref


def put_left(window_ref, base, side, ref):
    for j in range(3):
        high, low = split(ref[j])
        for part, value in enumerate((high, low, high)):
            window_ref[base + j, :, 16 * side : 16 * side + 16, lanes(part)] = value


def square_first_kernel(
    place_ref, given, total_ref, rest_ref, window_ref, right_ref
):
    slabs, rows = given[:8], given[8:]
    blank_corners(right_ref, 13)
    total_ref[...] = jnp.zeros_like(total_ref)
    for n, wait in enumerate(slabs):
        at = place_ref[5 + n] * 16
        put_right(right_ref, ((at, True), (128 + at, True), (256 + at, False)), wait())
    for n in range(4):
        for side in range(2):
            put_left(window_ref, 3 * n, side, rows[2 * n + side]())
        firsts = [place_ref[n] * 3 + j for j in range(3)]
        pieces = (
            (window_ref[3 * n + j].reshape(13 * 32, 384), right_ref[r])
            for j, r in enumerate(firsts)
        )
        accumulate(pieces, total_ref, 32, firsts)
    for j in range(3):
        rest_ref[j] = right_ref[place_ref[4] * 3 + j]


def square_second_kernel(place_ref, mask_ref, given, out_ref, window_ref, total_ref):
    before, rest, beside_o, beside_m = given
    put_left(window_ref, 0, 0, beside_o())
    put_left(window_ref, 0, 1, beside_m())
    right_ref = rest()
    total_ref[...] = before()[...]
    firsts = [place_ref[4] * 3 + j for j in range(3)]
    pieces = ((window_ref[j].reshape(13 * 32, 384), right_ref[j]) for j in range(3))
    accumulate(pieces, total_ref, 32, firsts)
    for g in range(3):
        for e in range(19):
            kept = mask_ref[g, e].astype(F32)
            for side in range(2):
                out_ref[side, g, e] = total_ref[g, e + 5, 16 * side : 16 * side + 16] * kept


def quartet(low_y):
    return low_y, 3 - low_y, low_y ^ 1, (3 - low_y) ^ 1


def fill_half(right_ref, chips, slabs, core):
    blank_corners(right_ref, 19)
    zero = jnp.zeros((21, 16, 384), BF16)
    for chip, slab in zip(chips, slabs):
        place = 32 * chip + 16 * core
        idle = 128 + 32 * chip + 16 * (1 - core)
        right_ref[:, pl.ds(pl.multiple_of(idle, 16), 16), :] = zero
        again = lax.rem(place + 16, 128)
        put_right(right_ref, ((place, True), (again, True), (128 + place, False)), slab())


def cube_first_kernel(place_ref, given, total_ref, next_ref, window_ref, right_ref):
    rows, slabs = given[:7], given[7:]
    low_y, core = place_ref[7], place_ref[8]
    fill_half(right_ref, quartet(low_y), slabs, core)
    mine = lax.broadcasted_iota(jnp.int32, (208, 128), 1) // 16 % 2 == core
    blocks = window_ref.shape[1:3] + (128,)
    for n, wait in enumerate(rows):
        base = place_ref[n] * 3
        ref = wait()
        for j in range(3):
            values = ref[j].reshape(208, 128)
            rounded = values.astype(BF16)
            high = rounded.astype(F32)
            low = pltpu.roll(values - high, 16, 1)
            first = jnp.where(mine, high, low).astype(BF16)
            second = jnp.where(mine, low, high).astype(BF16)
            window_ref[base + j, :, :, lanes(0)] = first.reshape(blocks)
            window_ref[base + j, :, :, lanes(1)] = rounded.reshape(blocks)
            next_ref[base + j, :, :, lanes(0)] = second.reshape(blocks)
            next_ref[base + j, :, :, lanes(1)] = rounded.reshape(blocks)
    total_ref[...] = jnp.zeros_like(total_ref)
    all_rows(window_ref, right_ref, total_ref)


def cube_second_kernel(place_ref, mask_ref, given, out_ref, right_ref, total_ref):
    before, window, own, slabs = given[0], given[1], given[2], given[3:]
    low_y, core = place_ref[7], place_ref[8]
    fill_half(right_ref, quartet(low_y), slabs, 1 - core)
    total_ref[...] = before()[...]
    window_ref, own_ref = window(), own()
    all_rows(window_ref, right_ref, total_ref)
    for g in range(3):
        for f in range(25):
            value = -2.0 * total_ref[g, f + 5]
            if 3 <= f < 22:
                value = 3.0 * own_ref[g, f - 3] + value
            out_ref[g, f] = value * mask_ref[g, f].astype(F32)


SMEM = pl.BlockSpec(memory_space=pltpu.SMEM)
VMEM = pl.BlockSpec(memory_space=pltpu.VMEM)
IN_HBM = pl.BlockSpec(memory_space=pltpu.HBM)
MIB = 1024 * 1024
LARGE, SMALL = 60, 24


def call(kernel, scalars, given, out_shape, scratch, limit, fetch):
    arrays, views, held = [], [], []
    for item in given:
        array, part = item if isinstance(item, tuple) else (item, None)
        known = [n for n, other in enumerate(arrays) if other is array]
        if not known:
            arrays.append(array)
        views.append((known[0] if known else len(arrays) - 1, part))
        held.append(pltpu.VMEM(array.shape if part is None else array.shape[1:], array.dtype))
    first = len(scalars)
    last = first + len(arrays)
    extra = held + [pltpu.SemaphoreType.DMA((len(held),))] if fetch else []

    def whole(*refs):
        parts = [refs[first + n] if p is None else refs[first + n].at[p] for n, p in views]
        end = len(refs) - len(extra)
        waits = fetched(parts, refs[end:-1], refs[-1]) if fetch else [here(p) for p in parts]
        kernel(*refs[:first], waits, *refs[last:end])

    return pl.pallas_call(
        whole,
        out_shape=out_shape,
        in_specs=[SMEM] * first + [IN_HBM if fetch else VMEM] * len(arrays),
        out_specs=jax.tree.map(lambda _: VMEM, out_shape),
        scratch_shapes=scratch + extra,
        compiler_params=pltpu.CompilerParams(vmem_limit_bytes=limit * MIB),
        cost_estimate=pl.CostEstimate(flops=1000000, bytes_accessed=1000, transcendentals=0),
    )(*scalars, *arrays)


def body(x_band, x_mask, sq_mask, cube_mask):
    high_y = lax.axis_index("row") % 2
    low_y, core = lax.axis_index("col") // 2, lax.axis_index("col") % 2

    own = pl.pallas_call(
        mask_kernel,
        out_shape=jax.ShapeDtypeStruct(x_band.shape, F32),
        in_specs=[SMEM, VMEM],
        out_specs=VMEM,
    )(x_mask, x_band)

    own_m, pair_m, below_o, above_o = together(
        send(own, MIRROR), send(own, FLIP), send(own, UP), send(own, DOWN)
    )
    both = jnp.stack([own, own_m])
    pair_o = send(own_m, FLIP)
    after, twin = send(both, NEXT), send(both, SIBLING)
    pair_o, below_m, above_m = together(pair_o, send(own_m, UP), send(own_m, DOWN))
    after, beside_m = together(after, send(pair_m, ACROSS))
    beside_o, twin_after = send(pair_o, ACROSS), send(after, SIBLING)

    chips = jnp.stack([low_y, 3 - low_y, low_y ^ 1, (3 - low_y) ^ 1])
    orbitals = jnp.concatenate([2 * chips + core, 2 * chips + 1 - core])
    pair_at, beside_at = 3 - 2 * high_y, 1 + 2 * high_y
    square_rows = jnp.stack([jnp.int32(0), jnp.int32(4), jnp.int32(2), pair_at, beside_at])
    square_places = jnp.concatenate([square_rows, orbitals]).astype(jnp.int32)
    cube_places = [1, 5, 3, pair_at + 1, beside_at + 1, 6 - 6 * high_y, 6 * high_y, low_y, core]
    cube_places = jnp.stack([jnp.int32(v) for v in cube_places])

    left = [(array, part) for array in (both, after, twin, twin_after) for part in (0, 1)]

    partial, rest = call(
        square_first_kernel,
        (square_places,),
        left + [below_o, below_m, above_o, above_m, (both, 0), (both, 1), pair_o, pair_m],
        (
            jax.ShapeDtypeStruct((3, 29, 32, 128), F32),
            jax.ShapeDtypeStruct((3, 384, 384), BF16),
        ),
        [pltpu.VMEM((12, 13, 32, 384), BF16), pltpu.VMEM((15, 384, 384), BF16)],
        LARGE,
        True,
    )
    square = call(
        square_second_kernel,
        (square_places, sq_mask),
        [partial, rest, beside_o, beside_m],
        jax.ShapeDtypeStruct((2, 3, 19, 16, 128), F32),
        [pltpu.VMEM((3, 13, 32, 384), BF16), pltpu.VMEM((3, 29, 32, 128), F32)],
        SMALL,
        False,
    )
    square_twin = send(square, SIBLING)
    square_after, far_a, far_b = together(
        send(square, NEXT), send(pair_o, AGAINST), send(beside_o, ACROSS)
    )
    total, window = call(
        cube_first_kernel,
        (cube_places,),
        [below_o, above_o, (both, 0), pair_o, beside_o, far_a, far_b]
        + [(square, 0), (square, 1), (square_after, 0), (square_after, 1)],
        (
            jax.ShapeDtypeStruct((3, 35, 16, 128), F32),
            jax.ShapeDtypeStruct((21, 13, 16, 256), BF16),
        ),
        [pltpu.VMEM((21, 13, 16, 256), BF16), pltpu.VMEM((21, 256, 384), BF16)],
        SMALL,
        False,
    )
    after_twin = send(square_after, SIBLING)
    return call(
        cube_second_kernel,
        (cube_places, cube_mask),
        [total, window, (square, 0), (square_twin, 0), (square_twin, 1)]
        + [(after_twin, 0), (after_twin, 1)],
        jax.ShapeDtypeStruct((3, 25, 16, 128), F32),
        [pltpu.VMEM((21, 256, 384), BF16), pltpu.VMEM((3, 35, 16, 128), F32)],
        SMALL,
        False,
    )


def solution(mesh):
    return jax.shard_map(
        body,
        mesh=mesh,
        in_specs=(P("row", None, "col", None), P("row", None), P("row", None), P("row", None)),
        out_specs=P("row", None, "col", None),
        check_vma=False,
    )
```
